256 devices in a mesh: row: 16 (over z, core), col: 16 (over y, x).
Axes of the slice: x: 4, y: 4, z: 8, core: 2. Of those that a mesh axis runs over, the one named last changes fastest.
Arguments:
- tokens: bfloat16 [1024, 12288], P('col', 'row'), may hold values from -120 to 120, as said below
- norm_gain: float32 [12288], P('row'), may hold values from 0.1 to 1.9
- norm_bias: float32 [12288], P('row'), may hold values from -3 to 3
- weight_in: bfloat16 [12288, 49152], P('row', 'col'), may hold values from -0.0546875 to 0.0546875
- bias_in: float32 [49152], P('col'), may hold values from -3 to 3
- weight_out: bfloat16 [49152, 12288], P('col', 'row'), may hold values from -0.02734375 to 0.02734375
- bias_out: float32 [12288], P('row'), may hold values from -3 to 3
Outputs:
- block_out: bfloat16 [1024, 12288], P('col', 'row')
The draws below stay inside these ranges and needn't reach their ends.
Inputs may be any that keep to these rules, and one draw needn't show every extreme that they name: `tokens`: real-valued activations.
All inputs are finite; a program needn't handle non-finite values.
Results may differ from the reference program's by a relative error of at most 0.0075.
Values may be sent and summed in bfloat16 or wider, within the bound.
No kernel may reach another device: no remote copies, remote signals or barrier semaphores. Data moves between devices by JAX's collectives and lax.ppermute only.
A program may use at most 64 MiB of HBM per device.

```python
import jax
import jax.numpy as jnp
from jax import lax

D = 12288
FF = 49152
TOKENS = 1024
N_ROW = 16
N_COL = 16


def draw_tokens(key, part):
    key = jax.random.fold_in(key, 1)
    key_base = jax.random.fold_in(key, 0)
    key_rows = jax.random.fold_in(key, 1)
    key_cols = jax.random.fold_in(key, 2)
    key_levels = jax.random.fold_in(key, 4)
    key_shift = jax.random.fold_in(key, 5)
    block_width = D // N_ROW
    ranks = jax.random.permutation(key_levels, N_ROW).astype(jnp.float32)
    level_exp = ranks / max(N_ROW - 1, 1) * 1.5 - 0.75
    block_level = 10.0 ** level_exp
    block_shift = jax.random.uniform(key_shift, (N_ROW,), jnp.float32, -0.5, 1.5)
    rough = jnp.exp(jax.random.uniform(key_cols, (D,), jnp.float32, -0.25, 0.25))
    col_scale = jnp.repeat(block_level, block_width) * rough
    col_shift = jnp.repeat(block_shift, block_width)
    base = jnp.clip(jax.random.normal(key_base, (TOKENS, D), jnp.float32), -3.5, 3.5)
    base = base + col_shift[None, :]
    row_scale = 10.0 ** jax.random.uniform(key_rows, (TOKENS,), jnp.float32, -0.5, 0.5)
    values = base * row_scale[:, None] * col_scale[None, :]
    return values.astype(jnp.bfloat16)


def levels(rng, shape, pieces, low, high):
    gain, own = 1.0, jax.random.fold_in(rng, 6)
    for dim, parts in pieces:
        heights = jnp.exp(jax.random.uniform(jax.random.fold_in(own, dim), (parts,), jnp.float32, low / len(pieces), high / len(pieces)))
        gain = gain * jnp.repeat(heights, shape[dim] // parts).reshape([-1 if axis == dim else 1 for axis in range(len(shape))])
    return gain


def centred(rng, shape, deviation, reach, pieces=(), dtype=jnp.bfloat16):
    factor_of = levels(rng, shape, pieces, -0.22, 0.18) if pieces else 1.0
    values = jax.random.normal(rng, shape, jnp.float32) * deviation * factor_of
    return jnp.minimum(jnp.maximum(values, -reach), reach).astype(dtype)


def setup_inputs(seed: int = 0) -> dict:
    key_of = jax.random.split(jax.random.key(seed), 8)
    tokens = draw_tokens(jax.random.fold_in(key_of[7], 71), 0)
    norm_gain = jnp.clip(1.0 + 0.18 * jax.random.normal(key_of[1], (D,), jnp.float32), 0.1, 1.9)
    norm_bias = centred(key_of[2], (D,), 0.5, 3.0, ((0, 16),), jnp.float32)
    weight_in = centred(key_of[3], (D, FF), D ** -0.5, 0.0546875, ((0, 16), (1, 16)))
    bias_in = centred(key_of[4], (FF,), 0.5, 3.0, ((0, 16),), jnp.float32)
    weight_out = centred(key_of[5], (FF, D), FF ** -0.5, 0.02734375, ((0, 16), (1, 16)))
    bias_out = centred(key_of[6], (D,), 0.5, 3.0, ((0, 16),), jnp.float32)
    return {"tokens": tokens, "norm_gain": norm_gain, "norm_bias": norm_bias, "weight_in": weight_in, "bias_in": bias_in, "weight_out": weight_out, "bias_out": bias_out}


epsilon = 1e-05

def reference(tokens, norm_gain, norm_bias, weight_in, bias_in, weight_out, bias_out):
    floats = tokens.astype(jnp.float32)
    center = lax.optimization_barrier(jnp.mean(floats, axis=1))
    differ = floats - center[:, None]
    variance = lax.optimization_barrier(jnp.mean(differ * differ, axis=1))
    normed = (differ * lax.rsqrt(variance + epsilon)[:, None] * norm_gain + norm_bias).astype(jnp.bfloat16)
    feat_block = D // N_ROW
    normed_blocks = normed.reshape(TOKENS, N_ROW, feat_block).transpose(1, 0, 2)
    in_blocks = weight_in.reshape(N_ROW, feat_block, FF)

    def first_step(carry, pair):
        block_term = jnp.dot(pair[0], pair[1], preferred_element_type=jnp.float32)
        return (carry + block_term.astype(jnp.bfloat16).astype(jnp.float32), None)
    preact, _ = lax.scan(first_step, jnp.zeros((TOKENS, FF), jnp.float32), (normed_blocks, in_blocks))
    hidden = jax.nn.gelu(preact + bias_in, approximate=True).astype(jnp.bfloat16)
    hid_block = FF // N_COL
    hidden_blocks = hidden.reshape(TOKENS, N_COL, hid_block).transpose(1, 0, 2)
    out_blocks = weight_out.reshape(N_COL, hid_block, D)
    outsum, _ = lax.scan(first_step, jnp.zeros((TOKENS, D), jnp.float32), (hidden_blocks, out_blocks))
    return (outsum + bias_out + floats).astype(jnp.bfloat16)
```

```python
import jax
import jax.numpy as jnp
from jax import lax
from jax.sharding import Mesh
from jax.sharding import PartitionSpec as P

epsilon = 1e-05
sizes = {"z": 8, "core": 2, "y": 4, "x": 4}
parts = 2


def shift(value, axis, distance):
    size = sizes[axis]
    return lax.ppermute(value, axis, [(i, (i + distance) % size) for i in range(size)])


def put(into, block, index):
    return lax.dynamic_update_index_in_dim(into, block, index, 0)


def add(*terms):
    total = terms[0].astype(jnp.float32)
    for term in terms[1:]:
        total = total + term.astype(jnp.float32)
    return total


def statistics(floats):
    block = floats.shape[1]
    mean = jnp.sum(floats, axis=1) / block
    differ = floats - mean[:, None]
    squares = jnp.sum(differ * differ, axis=1)
    mine = jnp.stack([mean, squares])
    other = shift(mine, "core", 1)
    gap = mine[0] - other[0]
    pair = jnp.stack([0.5 * (mine[0] + other[0]), mine[1] + other[1] + 0.5 * block * gap * gap])
    pairs = jnp.stack([pair] + [shift(pair, "z", d) for d in range(1, sizes["z"])])
    center = jnp.mean(pairs[:, 0], axis=0)
    away = pairs[:, 0] - center
    total = jnp.sum(pairs[:, 1], axis=0) + 2 * block * jnp.sum(away * away, axis=0)
    return center, total / (2 * block * sizes["z"])


def gather_plane(block):
    for axis in ("x", "y"):
        here = lax.axis_index(axis)
        size = sizes[axis]
        whole = jnp.zeros((size,) + block.shape, block.dtype)
        whole = put(whole, block, here)
        for distance in (1, -1, 2):
            whole = put(whole, shift(block, axis, distance), lax.rem(here - distance + size, size))
        block = whole
    return block


def scatter_ring(share):
    here, size = lax.axis_index("z"), sizes["z"]
    half = share.shape[1] // 2

    def at(offset):
        return lax.dynamic_index_in_dim(share, lax.rem(here + offset + size, size), 0, keepdims=False)

    far = at(4)
    right, left = shift(far[:half], "z", 1), shift(far[half:], "z", -1)
    one, two = at(3), at(-3)
    right = jnp.concatenate([add(one[:half], right).astype(jnp.bfloat16), one[half:]])
    left = jnp.concatenate([two[:half], add(two[half:], left).astype(jnp.bfloat16)])
    for offset in (2, 1):
        right, left = shift(right, "z", 1), shift(left, "z", -1)
        right = add(at(offset), right).astype(jnp.bfloat16)
        left = add(at(-offset), left).astype(jnp.bfloat16)
    right, left = shift(right, "z", 1), shift(left, "z", -1)
    return add(at(0), right, left)


def gather_ring(tile):
    here, size = lax.axis_index("z"), sizes["z"]
    half = tile.shape[0] // 2
    whole = jnp.zeros((size,) + tile.shape, tile.dtype)
    whole = put(whole, tile, here)
    right = left = tile
    for distance in (1, 2, 3):
        right, left = shift(right, "z", 1), shift(left, "z", -1)
        whole = put(whole, right, lax.rem(here - distance + size, size))
        whole = put(whole, left, lax.rem(here + distance, size))
    right, left = shift(right[:half], "z", 1), shift(left[half:], "z", -1)
    return put(whole, jnp.concatenate([right, left]), lax.rem(here + 4, size))


def body(tokens, norm_gain, norm_bias, weight_in, bias_in, weight_out, bias_out):
    core = lax.axis_index("core")
    floats = tokens.astype(jnp.float32)
    center, variance = statistics(floats)
    differ = floats - center[:, None]
    normed = (differ * lax.rsqrt(variance + epsilon)[:, None] * norm_gain + norm_bias).astype(
        jnp.bfloat16
    )
    rows = tokens.shape[0] // parts
    features = tokens.shape[1]
    units = weight_in.shape[1]
    outs = []
    for part in range(parts):
        mine = normed[part * rows : (part + 1) * rows]
        gathered = gather_plane(mine).reshape(sizes["z"], 2, rows, features)

        def product(which):
            block = lax.dynamic_index_in_dim(gathered, which, 1, keepdims=False)
            return jnp.dot(
                block.reshape(-1, features), weight_in, preferred_element_type=jnp.float32
            )

        sent = shift(product(1 - core).astype(jnp.bfloat16), "core", 1)
        share = add(product(core), sent).astype(jnp.bfloat16).reshape(sizes["z"], rows, units)
        preact = scatter_ring(share) + bias_in
        hidden = jax.nn.gelu(preact, approximate=True).astype(jnp.bfloat16)
        own = gather_ring(hidden).reshape(-1, units)
        other = shift(own, "core", 1)

        def second(lhs):
            value = jnp.dot(lhs, weight_out, preferred_element_type=jnp.float32)
            return value.astype(jnp.bfloat16).reshape(sizes["z"], 1, rows, features)

        one, two = second(own), second(other)
        first = jnp.where(core == 0, one, two)
        last = jnp.where(core == 0, two, one)
        blocks = jnp.concatenate([first, last], axis=1).reshape(-1, rows, features)
        arrived = lax.all_to_all(blocks, ("y", "x"), 0, 0, tiled=True)
        summed = jnp.sum(arrived.astype(jnp.float32), axis=0)
        outs.append(summed + bias_out + floats[part * rows : (part + 1) * rows])
    return jnp.concatenate(outs).astype(jnp.bfloat16)


def solution(mesh):
    fine = Mesh(mesh.devices.reshape(8, 2, 4, 4), ("z", "core", "y", "x"))
    row, col = ("z", "core"), ("y", "x")
    placed = (P(col, row), P(row), P(row), P(row, col), P(col), P(col, row), P(row))
    return jax.shard_map(
        body, mesh=fine, in_specs=placed, out_specs=P(col, row), check_vma=False
    )
```

```python
import jax
import jax.numpy as jnp
from jax import lax
from jax.experimental import pallas as pl
from jax.experimental.pallas import tpu as pltpu
from jax.sharding import Mesh
from jax.sharding import PartitionSpec as P

epsilon = 1e-05
planes = 8
parts = 2
plane = ("y", "x")
megabyte = 2**20


def swap(value):
    return lax.ppermute(value, "core", [(0, 1), (1, 0)])


def onward(value, distance=1):
    pairs = []
    for z in range(planes):
        pairs.append((2 * z, 2 * ((z + distance) % planes)))
        pairs.append((2 * z + 1, 2 * ((z - distance) % planes) + 1))
    return lax.ppermute(value, ("z", "core"), pairs)


def add(*terms):
    total = terms[0].astype(jnp.float32)
    for term in terms[1:]:
        total = total + term.astype(jnp.float32)
    return total


def low(*terms):
    return add(*terms).astype(jnp.bfloat16)


def gather_tops(tops):
    pair = jnp.stack([tops, swap(tops)])
    near = [onward(pair, distance) for distance in (1, 2, 3)]
    near.append(onward(tops, 4)[None])
    near = jnp.concatenate(near)
    return pair, near, swap(near)


def block_index(z, steps, which):
    return 2 * lax.rem(z + steps + planes, planes) + which


def near_and_far(z, core):
    way = 1 - 2 * core
    out = [(0, core), (0, 1 - core)]
    for steps in (1, 2, 3):
        out += [(-way * steps, core), (-way * steps, 1 - core)]
    out.append((4, core))
    for steps in (1, 2, 3):
        out += [(way * steps, 1 - core), (way * steps, core)]
    out.append((4, 1 - core))
    return [block_index(z, steps, which) for steps, which in out]


def first_kernel(place, gathered, gain, weight, *refs):
    theirs, ours, left, notes = refs[-4:]
    z, core = place[0], place[1]
    rows, features = gathered.shape[1:]
    way = 1 - 2 * core

    @pl.when(pl.program_id(0) == 0)
    def _():
        wanted = [block_index(z, 4, 1 - core)]
        for steps in (3, 2, 1):
            wanted.append(block_index(z, -way * steps, 1 - core))
            wanted.append(block_index(z, -way * steps, core))
        wanted.append(block_index(z, 4, core))
        for steps in (3, 2, 1, 0):
            wanted.append(block_index(z, way * steps, core))
            wanted.append(block_index(z, way * steps, 1 - core))
        lane = lax.broadcasted_iota(jnp.int32, (rows, 128), 1)
        kind = lax.div(lane, 16)
        here = lane - 16 * kind == 2 * z + core
        for slot, number in enumerate(wanted):
            span = slice(slot * rows, (slot + 1) * rows)
            block = gathered[number].astype(jnp.float32)
            mean = jnp.sum(block, axis=1, keepdims=True) / features
            differ = block - mean
            left[span] = (differ * gain[...]).astype(jnp.bfloat16)
            note = jnp.zeros((rows, 128), jnp.float32)
            squares = jnp.sum(differ * differ, axis=1, keepdims=True)
            for base, value in ((0, mean), (3, squares)):
                rest = jnp.broadcast_to(value, (rows, 128))
                for piece in range(3):
                    part = rest.astype(jnp.bfloat16).astype(jnp.float32)
                    note = jnp.where(kind == base + piece, part, note)
                    rest = rest - part
            notes[span] = jnp.where(here, note, 0.0).astype(jnp.bfloat16)

    value = jnp.dot(left[...], weight[...], preferred_element_type=jnp.float32)
    theirs[...] = value[: 7 * rows].astype(jnp.bfloat16)
    ours[...] = value[7 * rows :].astype(jnp.bfloat16)

    @pl.when(pl.program_id(0) == pl.num_programs(0) - 1)
    def _():
        theirs[:, -128:] = notes[: 7 * rows]
        ours[:, -128:] = notes[7 * rows :]


def first_product(place, gathered, part, gain, weight, *before):
    blocks, features = gathered.shape[0], gathered.shape[2]
    rows = gathered.shape[1] // parts
    units, step = weight.shape[1], 640
    return pl.pallas_call(
        first_kernel,
        grid=((units + 128) // step,),
        in_specs=[
            pl.BlockSpec(memory_space=pltpu.SMEM),
            pl.BlockSpec((blocks, rows, features), lambda i: (0, part, 0)),
            pl.BlockSpec((1, features), lambda i: (0, 0)),
            pl.BlockSpec((features, step), lambda i: (0, i)),
        ]
        + [pl.BlockSpec(memory_space=pl.ANY)] * len(before),
        out_specs=[
            pl.BlockSpec((7 * rows, step), lambda i: (0, i)),
            pl.BlockSpec((9 * rows, step), lambda i: (0, i)),
        ],
        out_shape=[
            jax.ShapeDtypeStruct((7 * rows, units + 128), jnp.bfloat16),
            jax.ShapeDtypeStruct((9 * rows, units + 128), jnp.bfloat16),
        ],
        scratch_shapes=[
            pltpu.VMEM((blocks * rows, features), jnp.bfloat16),
            pltpu.VMEM((blocks * rows, 128), jnp.bfloat16),
        ],
        compiler_params=pltpu.CompilerParams(vmem_limit_bytes=24 * megabyte),
        cost_estimate=pl.CostEstimate(
            flops=2 * blocks * rows * features * units,
            bytes_accessed=2 * (features * units + blocks * rows * (features + units)),
            transcendentals=0,
        ),
    )(place, gathered, gain.reshape(1, features), weight, *before)


def activate_kernel(place, ours, moving, other, pair, near, far, bias, *refs):
    out = refs[-1]
    z, core = place[0], place[1]
    rows, units = out.shape
    features = 768
    total = ours[...].astype(jnp.float32) + moving[...].astype(jnp.float32)
    total = total + other[...].astype(jnp.float32)
    notes, total = total[:, units:], total[:, :units]
    lane = lax.broadcasted_iota(jnp.int32, (rows, 128), 1)
    kind = lax.div(lane, 16)
    lane = lane - 16 * kind
    tops = [pair[0], pair[1]] + [near[i] for i in range(7)] + [far[i] for i in range(7)]
    means, squares = [], 0.0
    for number in near_and_far(z, core):
        mine = jnp.where(lane == number, notes, 0.0)
        means.append(jnp.sum(jnp.where(kind < 3, mine, 0.0), axis=1, keepdims=True))
        squares = squares + jnp.sum(jnp.where(kind >= 3, mine, 0.0), axis=1, keepdims=True)
    center = sum(means) / len(means)
    moved, biases = 0.0, bias[...]
    for mean, top in zip(means, tops):
        away = mean - center
        squares = squares + features * away * away
        moved = moved + away * top[0:1]
        biases = biases + top[1:2]
    scale = lax.rsqrt(squares / (len(means) * features) + epsilon)
    preact = (total + moved) * scale + biases
    out[...] = jax.nn.gelu(preact, approximate=True).astype(jnp.bfloat16)


def activate(place, ours, moving, other, tops, bias, *before):
    rows, wide = other.shape
    units = bias.shape[0]
    tops_specs = [pl.BlockSpec(top.shape, lambda i: (0, 0, 0)) for top in tops]
    return pl.pallas_call(
        activate_kernel,
        grid=(1,),
        in_specs=[
            pl.BlockSpec(memory_space=pltpu.SMEM),
            pl.BlockSpec((rows, wide), lambda i: (7, 0)),
            pl.BlockSpec((rows, wide), lambda i: (0, 0)),
            pl.BlockSpec((rows, wide), lambda i: (0, 0)),
        ]
        + tops_specs
        + [pl.BlockSpec((1, units), lambda i: (0, 0))]
        + [pl.BlockSpec(memory_space=pl.ANY)] * len(before),
        out_specs=pl.BlockSpec((rows, units), lambda i: (0, 0)),
        out_shape=jax.ShapeDtypeStruct((rows, units), jnp.bfloat16),
        compiler_params=pltpu.CompilerParams(vmem_limit_bytes=24 * megabyte),
        cost_estimate=pl.CostEstimate(
            flops=60 * rows * units, bytes_accessed=12 * rows * units, transcendentals=rows * units
        ),
    )(place, ours, moving, other, *tops, bias.reshape(1, units), *before)


def tops_kernel(gain, bias, weight, *refs):
    out = refs[-1]
    rows = []
    for value in (gain[...], bias[...]):
        for _ in range(3):
            piece = value.astype(jnp.bfloat16).astype(jnp.float32)
            rows.append(piece)
            value = value - piece
    rows += [jnp.zeros_like(rows[0])] * 10
    left = jnp.concatenate(rows).astype(jnp.bfloat16)
    value = jnp.dot(left, weight[...], preferred_element_type=jnp.float32)
    out[0:1] = value[0:1] + value[1:2] + value[2:3]
    out[1:2] = value[3:4] + value[4:5] + value[5:6]


def tops_product(gain, bias, weight, *before):
    features, units = weight.shape
    step = 512
    return pl.pallas_call(
        tops_kernel,
        grid=(units // step,),
        in_specs=[pl.BlockSpec((1, features), lambda i: (0, 0))] * 2
        + [pl.BlockSpec((features, step), lambda i: (0, i))]
        + [pl.BlockSpec(memory_space=pl.ANY)] * len(before),
        out_specs=pl.BlockSpec((2, step), lambda i: (0, i)),
        out_shape=jax.ShapeDtypeStruct((2, units), jnp.float32),
        cost_estimate=pl.CostEstimate(
            flops=32 * features * units, bytes_accessed=2 * features * units, transcendentals=0
        ),
    )(gain.reshape(1, features), bias.reshape(1, features), weight, *before)


def second_kernel(*refs):
    tiles, weight, out, total = refs[:-3], refs[-3], refs[-2], refs[-1]
    rows = out.shape[1]
    left = jnp.concatenate([tile[...] for tile in tiles])
    value = jnp.dot(left, weight[...], preferred_element_type=jnp.float32)

    @pl.when(pl.program_id(0) == 0)
    def _():
        total[...] = value

    @pl.when(pl.program_id(0) > 0)
    def _():
        total[...] += value

    @pl.when(pl.program_id(0) == pl.num_programs(0) - 1)
    def _():
        for slot in range(out.shape[0]):
            out[slot] = total[slot * rows : (slot + 1) * rows].astype(jnp.bfloat16)


def second_product(tiles, weight, rows):
    units, features = weight.shape
    step = 512
    tokens = sum(tile.shape[0] for tile in tiles)
    return pl.pallas_call(
        second_kernel,
        grid=(units // step,),
        in_specs=[pl.BlockSpec((tile.shape[0], step), lambda i: (0, i)) for tile in tiles]
        + [pl.BlockSpec((step, features), lambda i: (i, 0))],
        out_specs=pl.BlockSpec((tokens // rows, rows, features), lambda i: (0, 0, 0)),
        out_shape=jax.ShapeDtypeStruct((tokens // rows, rows, features), jnp.bfloat16),
        scratch_shapes=[pltpu.VMEM((tokens, features), jnp.float32)],
        compiler_params=pltpu.CompilerParams(vmem_limit_bytes=24 * megabyte),
        cost_estimate=pl.CostEstimate(
            flops=2 * tokens * features * units,
            bytes_accessed=2 * (features * units + tokens * (features + units)),
            transcendentals=0,
        ),
    )(*tiles, weight)


def last_kernel(place, *refs):
    tiles, weight, done, out, total = refs[:4], refs[4], refs[5:7], refs[7], refs[8]
    rows = tiles[0].shape[0]
    left = jnp.concatenate([tile[...] for tile in tiles])
    value = jnp.dot(left, weight[...], preferred_element_type=jnp.float32)
    numbers = near_and_far(place[0], place[1])
    ends = (numbers[8], numbers[15])
    others = numbers[:8] + numbers[9:15]

    @pl.when(pl.program_id(0) == 0)
    def _():
        total[...] = value
        for part in range(parts):
            for slot, number in enumerate(others):
                out[number, part * rows : (part + 1) * rows] = done[part][slot]

    @pl.when(pl.program_id(0) > 0)
    def _():
        total[...] += value

    @pl.when(pl.program_id(0) == pl.num_programs(0) - 1)
    def _():
        for part in range(parts):
            for slot, number in enumerate(ends):
                first = (2 * part + slot) * rows
                out[number, part * rows : (part + 1) * rows] = total[first : first + rows].astype(
                    jnp.bfloat16
                )


def last_product(place, tiles, weight, done):
    units, features = weight.shape
    rows, step = tiles[0].shape[0], 1024
    shape = (16, parts * rows, features)
    return pl.pallas_call(
        last_kernel,
        grid=(units // step,),
        in_specs=[pl.BlockSpec(memory_space=pltpu.SMEM)]
        + [pl.BlockSpec((rows, step), lambda i: (0, i)) for tile in tiles]
        + [pl.BlockSpec((step, features), lambda i: (i, 0))]
        + [pl.BlockSpec(value.shape, lambda i: (0, 0, 0)) for value in done],
        out_specs=pl.BlockSpec(shape, lambda i: (0, 0, 0)),
        out_shape=jax.ShapeDtypeStruct(shape, jnp.bfloat16),
        scratch_shapes=[pltpu.VMEM((len(tiles) * rows, features), jnp.float32)],
        compiler_params=pltpu.CompilerParams(vmem_limit_bytes=24 * megabyte),
        cost_estimate=pl.CostEstimate(
            flops=2 * len(tiles) * rows * features * units,
            bytes_accessed=2 * features * (units + 32 * parts * rows),
            transcendentals=0,
        ),
    )(place, *tiles, weight, *done)


def body(tokens, norm_gain, norm_bias, weight_in, bias_in, weight_out, bias_out):
    core, z = lax.axis_index("core"), lax.axis_index("z")
    place = jnp.stack([z, core]).astype(jnp.int32)
    rows = tokens.shape[0] // parts
    ready = jnp.broadcast_to(tokens[None], (16,) + tokens.shape)
    gathered = lax.all_to_all(ready, plane, 0, 0, tiled=True)
    tops = gather_tops(tops_product(norm_gain, norm_bias, weight_in, ready))

    def tile(value, number):
        return value[rows * (2 * number - 1) : rows * (2 * number + 1)]

    def spread(hidden):
        moving = jnp.concatenate([hidden, swap(hidden)])
        own, other = [moving], []
        for number in (1, 2, 3, 4):
            moving = onward(moving if number < 4 else moving[:rows])
            own.append(moving)
            other.append(swap(moving))
        return own + other

    before, hiddens = tops[2], []
    for part in range(parts):
        theirs, ours = first_product(place, gathered, part, norm_gain, weight_in, before)
        before = theirs
        theirs = swap(theirs)
        moving = onward(low(ours[:rows], theirs[:rows]))
        moving = jnp.concatenate([moving, jnp.zeros_like(moving)])
        for number in (1, 2, 3):
            moving = onward(low(tile(ours, number), tile(theirs, number), moving))
        other = swap(low(ours[8 * rows :], moving[rows:]))
        hiddens.append(activate(place, ours, moving, other, tops, bias_in))
    done, last = [], []
    for hidden in hiddens:
        tiles = spread(hidden)
        done.append(second_product(tiles[:4] + tiles[5:8], weight_out, rows))
        last += [tiles[4], tiles[8]]
    shares = last_product(place, last, weight_out, done)
    arrived = lax.all_to_all(shares, plane, 0, 0, tiled=True)
    return (add(jnp.sum(arrived.astype(jnp.float32), axis=0), tokens) + bias_out).astype(
        jnp.bfloat16
    )


def solution(mesh):
    fine = Mesh(mesh.devices.reshape(8, 2, 4, 4), ("z", "core", "y", "x"))
    row, col = ("z", "core"), ("y", "x")
    placed = (P(col, row), P(row), P(row), P(row, col), P(col), P(col, row), P(row))
    return jax.shard_map(
        body, mesh=fine, in_specs=placed, out_specs=P(col, row), check_vma=False
    )
```

```python
import functools

import jax
import jax.numpy as jnp
from jax import lax
from jax.experimental import pallas as pl
from jax.experimental.pallas import tpu as pltpu
from jax.sharding import Mesh
from jax.sharding import PartitionSpec as P

epsilon = 1e-05
planes = 8
parts = 2
group = 8
rows = 32
plane = ("y", "x")
megabyte = 2**20
whole = pl.BlockSpec(memory_space=pltpu.VMEM)
scalars = pl.BlockSpec(memory_space=pltpu.SMEM)
anywhere = pl.BlockSpec(memory_space=pl.ANY)


def swap(value):
    return lax.ppermute(value, "core", [(0, 1), (1, 0)])


def onward(value, distance=1):
    pairs = []
    for z in range(planes):
        pairs.append((2 * z, 2 * ((z + distance) % planes)))
        pairs.append((2 * z + 1, 2 * ((z - distance) % planes) + 1))
    return lax.ppermute(value, ("z", "core"), pairs)


def around(z, steps):
    return lax.rem(z + steps + planes, planes)


def near_and_far(z, core):
    way = 1 - 2 * core
    out = [(0, core), (0, 1 - core)]
    for steps in (1, 2, 3):
        out += [(-way * steps, core), (-way * steps, 1 - core)]
    out.append((4, core))
    for steps in (1, 2, 3):
        out += [(way * steps, 1 - core), (way * steps, core)]
    out.append((4, 1 - core))
    return [2 * around(z, steps) + which for steps, which in out]


def params(size):
    return pltpu.CompilerParams(vmem_limit_bytes=size * megabyte)


def copies_kernel(offsets, place, tokens, *refs):
    out = refs[-1]
    for slot, steps in enumerate(offsets):
        block = tokens[around(place[0], steps)]
        for i in range(out.shape[0]):
            out[i, slot] = block


def copies(offsets, place, tokens, *before):
    shape = (16, len(offsets)) + tokens.shape[1:]
    return pl.pallas_call(
        functools.partial(copies_kernel, offsets),
        in_specs=[scalars, whole] + [anywhere] * len(before),
        out_specs=whole,
        out_shape=jax.ShapeDtypeStruct(shape, tokens.dtype),
        compiler_params=params(16),
    )(place, tokens, *before)


def tops_kernel(gain, bias, weight, *refs):
    out = refs[-1]
    left = []
    for value in (gain[...], bias[...]):
        for _ in range(3):
            piece = value.astype(jnp.bfloat16).astype(jnp.float32)
            left.append(piece)
            value = value - piece
    left += [jnp.zeros_like(left[0])] * 10
    left = jnp.concatenate(left).astype(jnp.bfloat16)
    value = jnp.dot(left, weight[...], preferred_element_type=jnp.float32)
    out[0:1] = value[0:1] + value[1:2] + value[2:3]
    out[1:2] = value[3:4] + value[4:5] + value[5:6]


def tops_product(gain, bias, weight, *before):
    features, units = weight.shape
    step = 1536
    return pl.pallas_call(
        tops_kernel,
        grid=(units // step,),
        in_specs=[pl.BlockSpec((1, features), lambda i: (0, 0))] * 2
        + [pl.BlockSpec((features, step), lambda i: (0, i))]
        + [anywhere] * len(before),
        out_specs=pl.BlockSpec((2, step), lambda i: (0, i)),
        out_shape=jax.ShapeDtypeStruct((2, units), jnp.float32),
        compiler_params=params(24),
        cost_estimate=pl.CostEstimate(
            flops=32 * features * units, bytes_accessed=2 * features * units, transcendentals=0
        ),
    )(gain, bias, weight, *before)


def early_blocks(core):
    theirs, ours = [], []
    for part in range(parts):
        theirs += [(0, part, 1 - core), (2 - core, part, 1 - core), (2 - core, part, core)]
        ours += [(0, part, core), (1 + core, part, core), (1 + core, part, 1 - core)]
    return theirs, ours


def later_blocks(core):
    theirs, ours = [], []
    for part in range(parts):
        for first in (3, 5):
            theirs += [(first + 1 - core, part, 1 - core), (first + 1 - core, part, core)]
            ours += [(first + core, part, core), (first + core, part, 1 - core)]
        ours += [(7, part, core), (7, part, 1 - core)]
    return theirs, ours


def first_kernel(choose, place, gathered, gain, weight, *refs):
    theirs, ours, left, notes = refs[-4:]
    z, core = place[0], place[1]
    features = gathered.shape[-1]
    split = theirs.shape[0]

    lane = lax.broadcasted_iota(jnp.int32, (rows, 128), 1)
    kind = lax.div(lane, 16)
    here = lane - 16 * kind == 2 * z + core
    for slot, (number, part, which) in enumerate(sum(choose(core), [])):
        span = slice(slot * rows, (slot + 1) * rows)
        base = 8 * part + 4 * which
        block = jnp.concatenate(
            [gathered[base + i, number].astype(jnp.float32) for i in range(4)]
        )
        mean = jnp.sum(block, axis=1, keepdims=True) / features
        differ = block - mean
        left[span] = (differ * gain[...]).astype(jnp.bfloat16)
        note = jnp.zeros((rows, 128), jnp.float32)
        squares = jnp.sum(differ * differ, axis=1, keepdims=True)
        for first, value in ((0, mean), (3, squares)):
            rest = jnp.broadcast_to(value, (rows, 128))
            for piece in range(3):
                near = rest.astype(jnp.bfloat16).astype(jnp.float32)
                note = jnp.where(kind == first + piece, near, note)
                rest = rest - near
        notes[span] = jnp.where(here, note, 0.0).astype(jnp.bfloat16)
    theirs[:, -128:] = notes[:split]
    ours[:, -128:] = notes[split:]
    step = 768
    for first in range(0, weight.shape[1], step):
        span = slice(first, first + step)
        value = jnp.dot(left[...], weight[:, span], preferred_element_type=jnp.float32)
        theirs[:, span] = value[:split].astype(jnp.bfloat16)
        ours[:, span] = value[split:].astype(jnp.bfloat16)


def first_product(choose, place, gathered, gain, weight, *before):
    features, units = weight.shape
    split, rest = (rows * len(blocks) for blocks in choose(0))
    tokens = split + rest
    return pl.pallas_call(
        functools.partial(first_kernel, choose),
        in_specs=[scalars] + [whole] * 3 + [anywhere] * len(before),
        out_specs=[whole, whole],
        out_shape=[
            jax.ShapeDtypeStruct((split, units + 128), jnp.bfloat16),
            jax.ShapeDtypeStruct((rest, units + 128), jnp.bfloat16),
        ],
        scratch_shapes=[
            pltpu.VMEM((tokens, features), jnp.bfloat16),
            pltpu.VMEM((tokens, 128), jnp.bfloat16),
        ],
        compiler_params=params(24),
        cost_estimate=pl.CostEstimate(
            flops=2 * tokens * features * units,
            bytes_accessed=2 * (features * units + tokens * (features + units)),
            transcendentals=0,
        ),
    )(place, gathered, gain, weight, *before)


def sum_kernel(number, first, second, ours, theirs, moving, *refs):
    out = refs[-1]
    size = out.shape[0]
    total = ours[first * rows : first * rows + size].astype(jnp.float32)
    if number == 4:
        total = total + moving[rows:].astype(jnp.float32)
    else:
        total = total + theirs[second * rows : second * rows + size].astype(jnp.float32)
    if number in (2, 3):
        total = total + moving[...].astype(jnp.float32)
    if number == 1:
        out[:rows] = (total[:rows] + moving[...].astype(jnp.float32)).astype(jnp.bfloat16)
        out[rows:] = total[rows:].astype(jnp.bfloat16)
    else:
        out[...] = total.astype(jnp.bfloat16)


def ring_sum(number, first, second, ours, theirs, moving, *before):
    shape = (rows if number in (0, 4) else 2 * rows, ours.shape[1])
    return pl.pallas_call(
        functools.partial(sum_kernel, number, first, second),
        in_specs=[whole] * 3 + [anywhere] * len(before),
        out_specs=whole,
        out_shape=jax.ShapeDtypeStruct(shape, jnp.bfloat16),
        compiler_params=params(16),
        cost_estimate=pl.CostEstimate(
            flops=3 * shape[0] * shape[1], bytes_accessed=8 * shape[0] * shape[1], transcendentals=0
        ),
    )(ours, theirs, moving, *before)


def activate_kernel(features, first, place, ours, moving, other, pair, near, far, bias, out):
    units = out.shape[1]
    total = ours[first * rows : (first + 1) * rows].astype(jnp.float32)
    total = total + moving[:rows].astype(jnp.float32) + other[...].astype(jnp.float32)
    notes, total = total[:, units:], total[:, :units]
    lane = lax.broadcasted_iota(jnp.int32, (rows, 128), 1)
    kind = lax.div(lane, 16)
    lane = lane - 16 * kind
    tops = [pair[0], pair[1]] + [near[i] for i in range(7)] + [far[i] for i in range(7)]
    means, squares = [], 0.0
    for number in near_and_far(place[0], place[1]):
        mine = jnp.where(lane == number, notes, 0.0)
        means.append(jnp.sum(jnp.where(kind < 3, mine, 0.0), axis=1, keepdims=True))
        squares = squares + jnp.sum(jnp.where(kind >= 3, mine, 0.0), axis=1, keepdims=True)
    center = sum(means) / len(means)
    moved, biases = 0.0, bias[...]
    for mean, top in zip(means, tops):
        away = mean - center
        squares = squares + features * away * away
        moved = moved + away * top[0:1]
        biases = biases + top[1:2]
    scale = lax.rsqrt(squares / (len(means) * features) + epsilon)
    preact = (total + moved) * scale + biases
    out[...] = jax.nn.gelu(preact, approximate=True).astype(jnp.bfloat16)


def activate(features, first, place, ours, moving, other, tops, bias):
    units = bias.shape[1]
    return pl.pallas_call(
        functools.partial(activate_kernel, features, first),
        in_specs=[scalars] + [whole] * 7,
        out_specs=whole,
        out_shape=jax.ShapeDtypeStruct((rows, units), jnp.bfloat16),
        compiler_params=params(24),
        cost_estimate=pl.CostEstimate(
            flops=60 * rows * units, bytes_accessed=12 * rows * units, transcendentals=rows * units
        ),
    )(place, ours, moving, other, *tops, bias)


def half_kernel(moving, *refs):
    refs[-1][...] = moving[:rows]


def half(moving, *before):
    shape = (rows, moving.shape[1])
    return pl.pallas_call(
        half_kernel,
        in_specs=[whole] + [anywhere] * len(before),
        out_specs=whole,
        out_shape=jax.ShapeDtypeStruct(shape, moving.dtype),
        compiler_params=params(16),
    )(moving, *before)


def second_kernel(slots, place, *refs):
    tiles, weight, out = refs[:-2], refs[-2], refs[-1]
    left = jnp.concatenate([tile[...] for tile in tiles])
    total = jnp.dot(left, weight[...], preferred_element_type=jnp.float32)
    for slot, (number, part, which) in enumerate(slots(place[1])):
        base = 8 * part + 4 * which
        for i in range(4):
            first = slot * rows + i * group
            out[base + i, number] = total[first : first + group].astype(jnp.bfloat16)


def near_slots(core):
    out = []
    for part in range(parts):
        out += [(0, part, core), (0, part, 1 - core)]
        for steps in (1, 2):
            number = 2 * steps - 1 + core
            out += [(number, part, core), (number, part, 1 - core)]
        for steps in (1, 2):
            number = 2 * steps - core
            out += [(number, part, 1 - core), (number, part, core)]
    return out


def far_slots(core):
    out = []
    for part in range(parts):
        out += [(core, part, core), (core, part, 1 - core)]
        out += [(1 - core, part, 1 - core), (1 - core, part, core)]
        out += [(2, part, core), (2, part, 1 - core)]
    return out


def second_product(slots, groups, place, tiles, weight):
    units, features = weight.shape
    tokens = sum(tile.shape[0] for tile in tiles)
    return pl.pallas_call(
        functools.partial(second_kernel, slots),
        in_specs=[scalars] + [whole] * (len(tiles) + 1),
        out_specs=whole,
        out_shape=jax.ShapeDtypeStruct((16, groups, group, features), jnp.bfloat16),
        compiler_params=params(24),
        cost_estimate=pl.CostEstimate(
            flops=2 * tokens * features * units,
            bytes_accessed=2 * (features * units + tokens * (features + units)),
            transcendentals=0,
        ),
    )(place, *tiles, weight)


def last_kernel(place, near, far, tokens, bias, out):
    offsets = (0, -1, 1, -2, 2, -3, 3, 4)
    for slot, steps in enumerate(offsets):
        where = around(place[0], steps)
        total = tokens[where].astype(jnp.float32) + bias[...]
        for i in range(near.shape[0]):
            share = near[i, slot] if slot < 5 else far[i, slot - 5]
            total = total + share.astype(jnp.float32)
        out[where] = total.astype(jnp.bfloat16)


def last_sum(place, near, far, tokens, bias):
    return pl.pallas_call(
        last_kernel,
        in_specs=[scalars] + [whole] * 4,
        out_specs=whole,
        out_shape=jax.ShapeDtypeStruct(tokens.shape, tokens.dtype),
        compiler_params=params(24),
    )(place, near, far, tokens, bias)


def body(tokens, norm_gain, norm_bias, weight_in, bias_in, weight_out, bias_out):
    core, z = lax.axis_index("core"), lax.axis_index("z")
    place = jnp.stack([z, core]).astype(jnp.int32)
    features = tokens.shape[1]
    norm_gain, norm_bias = norm_gain.reshape(1, -1), norm_bias.reshape(1, -1)
    bias_in, bias_out = bias_in.reshape(1, -1), bias_out.reshape(1, -1)
    grouped = tokens.reshape(planes, group, features)

    def exchange(value):
        return lax.all_to_all(value, plane, 0, 0, tiled=True)

    ready = copies((4, 3, -3, 2, -2, 1, -1, 0), place, grouped)
    gathered = exchange(ready)
    mine = tops_product(norm_gain, norm_bias, weight_in, ready)
    pair = jnp.stack([mine, swap(mine)])
    near = [onward(pair, distance) for distance in (1, 2, 3)] + [onward(mine, 4)[None]]
    near = jnp.concatenate(near)
    far = swap(near)
    tops = pair, near, far

    theirs, ours = first_product(early_blocks, place, gathered, norm_gain, weight_in, far)
    theirs_later, ours_later = first_product(
        later_blocks, place, gathered, norm_gain, weight_in, theirs
    )
    theirs = swap(theirs)
    sent = [ring_sum(0, 3 * part, 3 * part, ours, theirs, theirs) for part in range(parts)]
    moving = [onward(value) for value in sent]
    for part in range(parts):
        first = 3 * part + 1
        moving[part] = onward(ring_sum(1, first, first, ours, theirs, moving[part]))
    theirs, ours = swap(theirs_later), ours_later
    hidden = []
    for part in range(parts):
        first, second = 6 * part, 4 * part
        step = moving[part]
        step = onward(ring_sum(2, first, second, ours, theirs, step))
        step = onward(ring_sum(3, first + 2, second + 2, ours, theirs, step))
        other = swap(ring_sum(4, first + 5, 0, ours, theirs, step))
        hidden.append(activate(features, first + 4, place, ours, step, other, tops, bias_in))

    tiles, last, steps = [], [], []
    for part in range(parts):
        step = jnp.concatenate([hidden[part], swap(hidden[part])])
        own = [step]
        for _ in range(2):
            step = onward(step)
            own.append(step)
        tiles += own + [swap(value) for value in own[1:]]
        steps.append(onward(step))
    shares = second_product(near_slots, 5, place, tiles, weight_out)
    near = exchange(shares)
    for step in steps:
        final = onward(half(step, shares))
        last += [step, swap(step), final, swap(final)]
    far = exchange(second_product(far_slots, 3, place, last, weight_out))
    out = last_sum(place, near, far, grouped, bias_out)
    return out.reshape(tokens.shape)


def solution(mesh):
    fine = Mesh(mesh.devices.reshape(8, 2, 4, 4), ("z", "core", "y", "x"))
    row, col = ("z", "core"), ("y", "x")
    placed = (P(col, row), P(row), P(row), P(row, col), P(col), P(col, row), P(row))
    return jax.shard_map(
        body, mesh=fine, in_specs=placed, out_specs=P(col, row), check_vma=False
    )
```

```python
import functools

import jax
import jax.numpy as jnp
from jax import lax
from jax.experimental import pallas as pl
from jax.experimental.pallas import tpu as pltpu
from jax.sharding import Mesh
from jax.sharding import PartitionSpec as P

epsilon = 1e-05
planes = 8
parts = 2
group = 8
rows = 32
plane = ("y", "x")
megabyte = 2**20
whole = pl.BlockSpec(memory_space=pltpu.VMEM)
scalars = pl.BlockSpec(memory_space=pltpu.SMEM)
anywhere = pl.BlockSpec(memory_space=pl.ANY)


def swap(value):
    return lax.ppermute(value, "core", [(0, 1), (1, 0)])


def onward(value, distance=1):
    pairs = []
    for z in range(planes):
        pairs.append((2 * z, 2 * ((z + distance) % planes)))
        pairs.append((2 * z + 1, 2 * ((z - distance) % planes) + 1))
    return lax.ppermute(value, ("z", "core"), pairs)


def around(z, steps):
    return lax.rem(z + steps + planes, planes)


def near_and_far(z, core):
    way = 1 - 2 * core
    out = [(0, core), (0, 1 - core)]
    for steps in (1, 2, 3):
        out += [(-way * steps, core), (-way * steps, 1 - core)]
    out.append((4, core))
    for steps in (1, 2, 3):
        out += [(way * steps, 1 - core), (way * steps, core)]
    out.append((4, 1 - core))
    return [2 * around(z, steps) + which for steps, which in out]


def params(size):
    return pltpu.CompilerParams(vmem_limit_bytes=size * megabyte)


def copies_kernel(offsets, place, tokens, *refs):
    out = refs[-1]
    for slot, steps in enumerate(offsets):
        block = tokens[around(place[0], steps)]
        for i in range(out.shape[0]):
            out[i, slot] = block


def copies(offsets, place, tokens, *before):
    shape = (16, len(offsets)) + tokens.shape[1:]
    return pl.pallas_call(
        functools.partial(copies_kernel, offsets),
        in_specs=[scalars, whole] + [anywhere] * len(before),
        out_specs=whole,
        out_shape=jax.ShapeDtypeStruct(shape, tokens.dtype),
        compiler_params=params(16),
    )(place, tokens, *before)


def tops_kernel(gain, bias, weight, *refs):
    out = refs[-1]
    left = []
    for value in (gain[...], bias[...]):
        for _ in range(3):
            piece = value.astype(jnp.bfloat16).astype(jnp.float32)
            left.append(piece)
            value = value - piece
    left += [jnp.zeros_like(left[0])] * 10
    left = jnp.concatenate(left).astype(jnp.bfloat16)
    value = jnp.dot(left, weight[...], preferred_element_type=jnp.float32)
    out[0:1] = value[0:1] + value[1:2] + value[2:3]
    out[1:2] = value[3:4] + value[4:5] + value[5:6]


def tops_product(gain, bias, weight, *before):
    features, units = weight.shape
    step = 1536
    return pl.pallas_call(
        tops_kernel,
        grid=(units // step,),
        in_specs=[pl.BlockSpec((1, features), lambda i: (0, 0))] * 2
        + [pl.BlockSpec((features, step), lambda i: (0, i))]
        + [anywhere] * len(before),
        out_specs=pl.BlockSpec((2, step), lambda i: (0, i)),
        out_shape=jax.ShapeDtypeStruct((2, units), jnp.float32),
        compiler_params=params(24),
        cost_estimate=pl.CostEstimate(
            flops=32 * features * units, bytes_accessed=2 * features * units, transcendentals=0
        ),
    )(gain, bias, weight, *before)


def early_blocks(core):
    theirs, ours = [], []
    for part in range(parts):
        theirs += [(0, part, 1 - core), (2 - core, part, 1 - core), (2 - core, part, core)]
        ours += [(0, part, core), (1 + core, part, core), (1 + core, part, 1 - core)]
    return theirs, ours


def later_blocks(core):
    theirs, ours = [], []
    for part in range(parts):
        for first in (3, 5):
            theirs += [(first + 1 - core, part, 1 - core), (first + 1 - core, part, core)]
            ours += [(first + core, part, core), (first + core, part, 1 - core)]
        ours += [(7, part, core), (7, part, 1 - core)]
    return theirs, ours


def first_kernel(choose, place, gathered, gain, weight, *refs):
    theirs, ours, left, notes = refs[-4:]
    z, core = place[0], place[1]
    features = gathered.shape[-1]
    split = theirs.shape[0]

    lane = lax.broadcasted_iota(jnp.int32, (rows, 128), 1)
    kind = lax.div(lane, 16)
    here = lane - 16 * kind == 2 * z + core
    for slot, (number, part, which) in enumerate(sum(choose(core), [])):
        span = slice(slot * rows, (slot + 1) * rows)
        base = 8 * part + 4 * which
        block = jnp.concatenate(
            [gathered[base + i, number].astype(jnp.float32) for i in range(4)]
        )
        mean = jnp.sum(block, axis=1, keepdims=True) / features
        differ = block - mean
        left[span] = (differ * gain[...]).astype(jnp.bfloat16)
        note = jnp.zeros((rows, 128), jnp.float32)
        squares = jnp.sum(differ * differ, axis=1, keepdims=True)
        for first, value in ((0, mean), (3, squares)):
            rest = jnp.broadcast_to(value, (rows, 128))
            for piece in range(3):
                near = rest.astype(jnp.bfloat16).astype(jnp.float32)
                note = jnp.where(kind == first + piece, near, note)
                rest = rest - near
        notes[span] = jnp.where(here, note, 0.0).astype(jnp.bfloat16)
    theirs[:, -128:] = notes[:split]
    ours[:, -128:] = notes[split:]
    step = 768
    for first in range(0, weight.shape[1], step):
        span = slice(first, first + step)
        value = jnp.dot(left[...], weight[:, span], preferred_element_type=jnp.float32)
        theirs[:, span] = value[:split].astype(jnp.bfloat16)
        ours[:, span] = value[split:].astype(jnp.bfloat16)


def first_product(choose, place, gathered, gain, weight, *before):
    features, units = weight.shape
    split, rest = (rows * len(blocks) for blocks in choose(0))
    tokens = split + rest
    return pl.pallas_call(
        functools.partial(first_kernel, choose),
        in_specs=[scalars] + [whole] * 3 + [anywhere] * len(before),
        out_specs=[whole, whole],
        out_shape=[
            jax.ShapeDtypeStruct((split, units + 128), jnp.bfloat16),
            jax.ShapeDtypeStruct((rest, units + 128), jnp.bfloat16),
        ],
        scratch_shapes=[
            pltpu.VMEM((tokens, features), jnp.bfloat16),
            pltpu.VMEM((tokens, 128), jnp.bfloat16),
        ],
        compiler_params=params(24),
        cost_estimate=pl.CostEstimate(
            flops=2 * tokens * features * units,
            bytes_accessed=2 * (features * units + tokens * (features + units)),
            transcendentals=0,
        ),
    )(place, gathered, gain, weight, *before)


def sum_kernel(number, first, second, ours, theirs, moving, *refs):
    out = refs[-1]
    size = out.shape[0]
    total = ours[first * rows : first * rows + size].astype(jnp.float32)
    if number == 4:
        total = total + moving[rows:].astype(jnp.float32)
    else:
        total = total + theirs[second * rows : second * rows + size].astype(jnp.float32)
    if number in (2, 3):
        total = total + moving[...].astype(jnp.float32)
    if number == 1:
        out[:rows] = (total[:rows] + moving[...].astype(jnp.float32)).astype(jnp.bfloat16)
        out[rows:] = total[rows:].astype(jnp.bfloat16)
    else:
        out[...] = total.astype(jnp.bfloat16)


def ring_sum(number, first, second, ours, theirs, moving, *before):
    shape = (rows if number in (0, 4) else 2 * rows, ours.shape[1])
    return pl.pallas_call(
        functools.partial(sum_kernel, number, first, second),
        in_specs=[whole] * 3 + [anywhere] * len(before),
        out_specs=whole,
        out_shape=jax.ShapeDtypeStruct(shape, jnp.bfloat16),
        compiler_params=params(16),
        cost_estimate=pl.CostEstimate(
            flops=3 * shape[0] * shape[1], bytes_accessed=8 * shape[0] * shape[1], transcendentals=0
        ),
    )(ours, theirs, moving, *before)


def activate_kernel(features, first, place, ours, moving, other, pair, near, far, bias, out):
    units = out.shape[1]
    total = ours[first * rows : (first + 1) * rows].astype(jnp.float32)
    total = total + moving[:rows].astype(jnp.float32) + other[...].astype(jnp.float32)
    notes, total = total[:, units:], total[:, :units]
    lane = lax.broadcasted_iota(jnp.int32, (rows, 128), 1)
    kind = lax.div(lane, 16)
    lane = lane - 16 * kind
    tops = [pair[0], pair[1]] + [near[i] for i in range(7)] + [far[i] for i in range(7)]
    means, squares = [], 0.0
    for number in near_and_far(place[0], place[1]):
        mine = jnp.where(lane == number, notes, 0.0)
        means.append(jnp.sum(jnp.where(kind < 3, mine, 0.0), axis=1, keepdims=True))
        squares = squares + jnp.sum(jnp.where(kind >= 3, mine, 0.0), axis=1, keepdims=True)
    center = sum(means) / len(means)
    moved, biases = 0.0, bias[...]
    for mean, top in zip(means, tops):
        away = mean - center
        squares = squares + features * away * away
        moved = moved + away * top[0:1]
        biases = biases + top[1:2]
    scale = lax.rsqrt(squares / (len(means) * features) + epsilon)
    preact = (total + moved) * scale + biases
    out[...] = jax.nn.gelu(preact, approximate=True).astype(jnp.bfloat16)


def activate(features, first, place, ours, moving, other, tops, bias):
    units = bias.shape[1]
    return pl.pallas_call(
        functools.partial(activate_kernel, features, first),
        in_specs=[scalars] + [whole] * 7,
        out_specs=whole,
        out_shape=jax.ShapeDtypeStruct((rows, units), jnp.bfloat16),
        compiler_params=params(24),
        cost_estimate=pl.CostEstimate(
            flops=60 * rows * units, bytes_accessed=12 * rows * units, transcendentals=rows * units
        ),
    )(place, ours, moving, other, *tops, bias)


def pass_kernel(value, *refs):
    out = refs[-1]
    out[...] = value[: out.shape[0]]


def passed(value, tokens, *before):
    return pl.pallas_call(
        pass_kernel,
        in_specs=[whole] + [anywhere] * len(before),
        out_specs=whole,
        out_shape=jax.ShapeDtypeStruct((tokens, value.shape[1]), value.dtype),
        compiler_params=params(16),
    )(value, *before)


def product_kernel(*refs):
    tiles, weight, out = refs[:-2], refs[-2], refs[-1]
    left = jnp.concatenate([tile[...] for tile in tiles])
    total = jnp.dot(left, weight[...], preferred_element_type=jnp.float32)
    out[...] = total.astype(jnp.bfloat16)


def merge_kernel(slots, earlier, place, *refs):
    done, weight, out = refs[0], refs[earlier], refs[-1]
    tiles = refs[earlier + 1 : -1]
    left = jnp.concatenate([tile[...] for tile in tiles])
    total = jnp.dot(left, weight[...], preferred_element_type=jnp.float32)
    old = new = 0
    for early, (number, part, which) in slots(place[1]):
        base = 8 * part + 4 * which
        for i in range(4):
            if early:
                first = old * rows + i * group
                out[base + i, number] = done[first : first + group]
            else:
                first = new * rows + i * group
                out[base + i, number] = total[first : first + group].astype(jnp.bfloat16)
        old, new = old + early, new + 1 - early


def near_slots(core):
    out = []
    for part in range(parts):
        out += [(0, (0, part, core)), (0, (0, part, 1 - core))]
        for steps in (1, 2):
            number = 2 * steps - 1 + core
            out += [(0, (number, part, core)), (0, (number, part, 1 - core))]
        for steps in (1, 2):
            number = 2 * steps - core
            out += [(0, (number, part, 1 - core)), (0, (number, part, core))]
    return out


def far_slots(core):
    out = []
    for part in range(parts):
        out += [(1, (core, part, core)), (1, (core, part, 1 - core))]
        out += [(1, (1 - core, part, 1 - core)), (1, (1 - core, part, core))]
    for part in range(parts):
        out += [(0, (2, part, core)), (0, (2, part, 1 - core))]
    return out


def second_cost(tokens, weight):
    units, features = weight.shape
    return pl.CostEstimate(
        flops=2 * tokens * features * units,
        bytes_accessed=2 * (features * units + tokens * (features + units)),
        transcendentals=0,
    )


def second_product(tiles, weight):
    tokens = sum(tile.shape[0] for tile in tiles)
    return pl.pallas_call(
        product_kernel,
        in_specs=[whole] * (len(tiles) + 1),
        out_specs=whole,
        out_shape=jax.ShapeDtypeStruct((tokens, weight.shape[1]), jnp.bfloat16),
        compiler_params=params(24),
        cost_estimate=second_cost(tokens, weight),
    )(*tiles, weight)


def merged_product(slots, groups, place, done, tiles, weight, *before):
    tokens = sum(tile.shape[0] for tile in tiles)

    def kernel(*refs):
        skipped = len(refs) - 1 - len(before)
        merge_kernel(slots, len(done), *refs[:skipped], refs[-1])

    return pl.pallas_call(
        kernel,
        in_specs=[scalars] + [whole] * (len(done) + 1 + len(tiles)) + [anywhere] * len(before),
        out_specs=whole,
        out_shape=jax.ShapeDtypeStruct((16, groups, group, weight.shape[1]), jnp.bfloat16),
        compiler_params=params(24),
        cost_estimate=second_cost(tokens, weight),
    )(place, *done, weight, *tiles, *before)


def base_kernel(tokens, bias, out):
    for i in range(tokens.shape[0]):
        out[i] = tokens[i].astype(jnp.float32) + bias[...]


def base_sum(tokens, bias):
    return pl.pallas_call(
        base_kernel,
        in_specs=[whole] * 2,
        out_specs=whole,
        out_shape=jax.ShapeDtypeStruct(tokens.shape, jnp.float32),
        compiler_params=params(16),
    )(tokens, bias)


def last_kernel(place, near, far, base, out):
    offsets = (0, -1, 1, -2, 2, -3, 3, 4)
    for slot, steps in enumerate(offsets):
        where = around(place[0], steps)
        total = base[where]
        for i in range(near.shape[0]):
            share = near[i, slot] if slot < 5 else far[i, slot - 5]
            total = total + share.astype(jnp.float32)
        out[where] = total.astype(jnp.bfloat16)


def last_sum(place, near, far, base):
    return pl.pallas_call(
        last_kernel,
        in_specs=[scalars] + [whole] * 3,
        out_specs=whole,
        out_shape=jax.ShapeDtypeStruct(base.shape, jnp.bfloat16),
        compiler_params=params(24),
    )(place, near, far, base)


def body(tokens, norm_gain, norm_bias, weight_in, bias_in, weight_out, bias_out):
    core, z = lax.axis_index("core"), lax.axis_index("z")
    place = jnp.stack([z, core]).astype(jnp.int32)
    features = tokens.shape[1]
    norm_gain, norm_bias = norm_gain.reshape(1, -1), norm_bias.reshape(1, -1)
    bias_in, bias_out = bias_in.reshape(1, -1), bias_out.reshape(1, -1)
    grouped = tokens.reshape(planes, group, features)

    def exchange(value):
        return lax.all_to_all(value, plane, 0, 0, tiled=True)

    ready = copies((4, 3, -3, 2, -2, 1, -1, 0), place, grouped)
    gathered = exchange(ready)
    mine = tops_product(norm_gain, norm_bias, weight_in, ready)
    pair = jnp.stack([mine, swap(mine)])
    near = [onward(pair, distance) for distance in (1, 2, 3)] + [onward(mine, 4)[None]]
    near = jnp.concatenate(near)
    far = swap(near)
    tops = pair, near, far

    theirs, ours = first_product(early_blocks, place, gathered, norm_gain, weight_in, far)
    theirs_later, ours_later = first_product(
        later_blocks, place, gathered, norm_gain, weight_in, theirs
    )
    theirs = swap(theirs)
    sent = [ring_sum(0, 3 * part, 3 * part, ours, theirs, theirs) for part in range(parts)]
    moving = [onward(value) for value in sent]
    for part in range(parts):
        first = 3 * part + 1
        moving[part] = onward(ring_sum(1, first, first, ours, theirs, moving[part]))
    theirs, ours = swap(theirs_later), ours_later
    hidden = []
    for part in range(parts):
        first, second = 6 * part, 4 * part
        step = moving[part]
        step = onward(ring_sum(2, first, second, ours, theirs, step))
        step = onward(ring_sum(3, first + 2, second + 2, ours, theirs, step))
        other = swap(ring_sum(4, first + 5, 0, ours, theirs, step))
        hidden.append(activate(features, first + 4, place, ours, step, other, tops, bias_in))

    base = base_sum(grouped, bias_out)
    tiles, steps = [], []
    for part in range(parts):
        step = jnp.concatenate([hidden[part], swap(hidden[part])])
        own = [step]
        for _ in range(2):
            step = onward(step)
            own.append(step)
        tiles += own + [swap(value) for value in own[1:]]
        steps.append(onward(step))
    near = merged_product(near_slots, 5, place, [], tiles, weight_out, base)
    four = [onward(passed(value, rows, near)) for value in steps]
    near = exchange(near)
    done = second_product([value for step in steps for value in (step, swap(step))], weight_out)
    four = [passed(value, rows, done) for value in four]
    far = [value for step in four for value in (step, swap(step))]
    far = merged_product(far_slots, 3, place, [done], far, weight_out)
    far = exchange(far)
    out = last_sum(place, near, far, base)
    return out.reshape(tokens.shape)


def solution(mesh):
    fine = Mesh(mesh.devices.reshape(8, 2, 4, 4), ("z", "core", "y", "x"))
    row, col = ("z", "core"), ("y", "x")
    placed = (P(col, row), P(row), P(row), P(row, col), P(col), P(col, row), P(row))
    return jax.shard_map(
        body, mesh=fine, in_specs=placed, out_specs=P(col, row), check_vma=False
    )
```

```python
import functools

import jax
import jax.numpy as jnp
from jax import lax
from jax.experimental import pallas as pl
from jax.experimental.pallas import tpu as pltpu
from jax.sharding import Mesh
from jax.sharding import PartitionSpec as P

epsilon = 1e-05
planes = 8
parts = 2
group = 8
rows = 32
plane = ("y", "x")
megabyte = 2**20
whole = pl.BlockSpec(memory_space=pltpu.VMEM)
scalars = pl.BlockSpec(memory_space=pltpu.SMEM)
anywhere = pl.BlockSpec(memory_space=pl.ANY)


def swap(value):
    return lax.ppermute(value, "core", [(0, 1), (1, 0)])


def onward(value, distance=1):
    pairs = []
    for z in range(planes):
        pairs.append((2 * z, 2 * ((z + distance) % planes)))
        pairs.append((2 * z + 1, 2 * ((z - distance) % planes) + 1))
    return lax.ppermute(value, ("z", "core"), pairs)


def around(z, steps):
    return lax.rem(z + steps + planes, planes)


def near_and_far(z, core):
    way = 1 - 2 * core
    out = [(0, core), (0, 1 - core)]
    for steps in (1, 2, 3):
        out += [(-way * steps, core), (-way * steps, 1 - core)]
    out.append((4, core))
    for steps in (1, 2, 3):
        out += [(way * steps, 1 - core), (way * steps, core)]
    out.append((4, 1 - core))
    return [2 * around(z, steps) + which for steps, which in out]


def params(size):
    return pltpu.CompilerParams(vmem_limit_bytes=size * megabyte)


def copies_kernel(offsets, place, tokens, *refs):
    out = refs[-1]
    for slot, steps in enumerate(offsets):
        block = tokens[around(place[0], steps)]
        for i in range(out.shape[0]):
            out[i, slot] = block


def copies(offsets, place, tokens, *before):
    shape = (16, len(offsets)) + tokens.shape[1:]
    return pl.pallas_call(
        functools.partial(copies_kernel, offsets),
        in_specs=[scalars, whole] + [anywhere] * len(before),
        out_specs=whole,
        out_shape=jax.ShapeDtypeStruct(shape, tokens.dtype),
        compiler_params=params(16),
    )(place, tokens, *before)


def tops_kernel(gain, bias, weight, *refs):
    out = refs[-1]
    left = []
    for value in (gain[...], bias[...]):
        for _ in range(3):
            piece = value.astype(jnp.bfloat16).astype(jnp.float32)
            left.append(piece)
            value = value - piece
    left += [jnp.zeros_like(left[0])] * 10
    left = jnp.concatenate(left).astype(jnp.bfloat16)
    value = jnp.dot(left, weight[...], preferred_element_type=jnp.float32)
    out[0:1] = value[0:1] + value[1:2] + value[2:3]
    out[1:2] = value[3:4] + value[4:5] + value[5:6]


def tops_product(gain, bias, weight, *before):
    features, units = weight.shape
    step = 1536
    return pl.pallas_call(
        tops_kernel,
        grid=(units // step,),
        in_specs=[pl.BlockSpec((1, features), lambda i: (0, 0))] * 2
        + [pl.BlockSpec((features, step), lambda i: (0, i))]
        + [anywhere] * len(before),
        out_specs=pl.BlockSpec((2, step), lambda i: (0, i)),
        out_shape=jax.ShapeDtypeStruct((2, units), jnp.float32),
        compiler_params=params(24),
        cost_estimate=pl.CostEstimate(
            flops=32 * features * units, bytes_accessed=2 * features * units, transcendentals=0
        ),
    )(gain, bias, weight, *before)


def early_blocks(core):
    theirs, ours = [], []
    for part in range(parts):
        theirs += [(0, part, 1 - core), (2 - core, part, 1 - core), (2 - core, part, core)]
        ours += [(0, part, core), (1 + core, part, core), (1 + core, part, 1 - core)]
    return theirs, ours


def later_blocks(core):
    theirs, ours = [], []
    for part in range(parts):
        for first in (3, 5):
            theirs += [(first + 1 - core, part, 1 - core), (first + 1 - core, part, core)]
            ours += [(first + core, part, core), (first + core, part, 1 - core)]
        ours += [(7, part, core), (7, part, 1 - core)]
    return theirs, ours


def first_kernel(choose, place, gathered, gain, weight, *refs):
    theirs, ours, left, notes = refs[-4:]
    z, core = place[0], place[1]
    features = gathered.shape[-1]
    split = theirs.shape[0]

    lane = lax.broadcasted_iota(jnp.int32, (rows, 128), 1)
    kind = lax.div(lane, 16)
    here = lane - 16 * kind == 2 * z + core
    for slot, (number, part, which) in enumerate(sum(choose(core), [])):
        span = slice(slot * rows, (slot + 1) * rows)
        base = 8 * part + 4 * which
        block = jnp.concatenate(
            [gathered[base + i, number].astype(jnp.float32) for i in range(4)]
        )
        mean = jnp.sum(block, axis=1, keepdims=True) / features
        differ = block - mean
        left[span] = (differ * gain[...]).astype(jnp.bfloat16)
        note = jnp.zeros((rows, 128), jnp.float32)
        squares = jnp.sum(differ * differ, axis=1, keepdims=True)
        for first, value in ((0, mean), (3, squares)):
            rest = jnp.broadcast_to(value, (rows, 128))
            for piece in range(3):
                near = rest.astype(jnp.bfloat16).astype(jnp.float32)
                note = jnp.where(kind == first + piece, near, note)
                rest = rest - near
        notes[span] = jnp.where(here, note, 0.0).astype(jnp.bfloat16)
    theirs[:, -128:] = notes[:split]
    ours[:, -128:] = notes[split:]

    def work(span):
        value = jnp.dot(left[...], weight[:, span], preferred_element_type=jnp.float32)
        theirs[:, span] = value[:split].astype(jnp.bfloat16)
        ours[:, span] = value[split:].astype(jnp.bfloat16)

    columns(weight.shape[1], 768, work)


def first_product(choose, place, gathered, gain, weight, *before):
    features, units = weight.shape
    split, rest = (rows * len(blocks) for blocks in choose(0))
    tokens = split + rest
    return pl.pallas_call(
        functools.partial(first_kernel, choose),
        in_specs=[scalars] + [whole] * 3 + [anywhere] * len(before),
        out_specs=[whole, whole],
        out_shape=[
            jax.ShapeDtypeStruct((split, units + 128), jnp.bfloat16),
            jax.ShapeDtypeStruct((rest, units + 128), jnp.bfloat16),
        ],
        scratch_shapes=[
            pltpu.VMEM((tokens, features), jnp.bfloat16),
            pltpu.VMEM((tokens, 128), jnp.bfloat16),
        ],
        compiler_params=params(24),
        cost_estimate=pl.CostEstimate(
            flops=2 * tokens * features * units,
            bytes_accessed=2 * (features * units + tokens * (features + units)),
            transcendentals=0,
        ),
    )(place, gathered, gain, weight, *before)


def columns(wide, step, work):
    def chunk(number, carry):
        work(pl.ds(pl.multiple_of(number * step, step), step))
        return carry

    lax.fori_loop(0, wide // step, chunk, 0)


def sum_kernel(number, first, second, ours, theirs, moving, *refs):
    out = refs[-1]
    size = out.shape[0]

    def work(span):
        total = ours[first * rows : first * rows + size, span].astype(jnp.float32)
        if number == 4:
            total = total + moving[rows:, span].astype(jnp.float32)
        else:
            share = theirs[second * rows : second * rows + size, span]
            total = total + share.astype(jnp.float32)
        if number in (2, 3):
            total = total + moving[:, span].astype(jnp.float32)
        if number == 1:
            near = total[:rows] + moving[:, span].astype(jnp.float32)
            out[:rows, span] = near.astype(jnp.bfloat16)
            out[rows:, span] = total[rows:].astype(jnp.bfloat16)
        else:
            out[:, span] = total.astype(jnp.bfloat16)

    columns(out.shape[1], 640, work)


def ring_sum(number, first, second, ours, theirs, moving, *before):
    shape = (rows if number in (0, 4) else 2 * rows, ours.shape[1])
    return pl.pallas_call(
        functools.partial(sum_kernel, number, first, second),
        in_specs=[whole] * 3 + [anywhere] * len(before),
        out_specs=whole,
        out_shape=jax.ShapeDtypeStruct(shape, jnp.bfloat16),
        compiler_params=params(16),
        cost_estimate=pl.CostEstimate(
            flops=3 * shape[0] * shape[1], bytes_accessed=8 * shape[0] * shape[1], transcendentals=0
        ),
    )(ours, theirs, moving, *before)


def activate_kernel(features, first, place, ours, moving, other, *refs):
    tops, bias, out = refs[:-2], refs[-2], refs[-1]
    units = out.shape[1]

    def sums(span):
        total = ours[first * rows : (first + 1) * rows, span].astype(jnp.float32)
        total = total + moving[:rows, span].astype(jnp.float32)
        return total + other[:, span].astype(jnp.float32)

    notes = sums(pl.ds(units, 128))
    lane = lax.broadcasted_iota(jnp.int32, (rows, 128), 1)
    kind = lax.div(lane, 16)
    lane = lane - 16 * kind
    tops = [top.at[i] for top in tops for i in range(top.shape[0])]
    means, squares = [], 0.0
    for number in near_and_far(place[0], place[1]):
        mine = jnp.where(lane == number, notes, 0.0)
        means.append(jnp.sum(jnp.where(kind < 3, mine, 0.0), axis=1, keepdims=True))
        squares = squares + jnp.sum(jnp.where(kind >= 3, mine, 0.0), axis=1, keepdims=True)
    center = sum(means) / len(means)
    away = [mean - center for mean in means]
    for value in away:
        squares = squares + features * value * value
    scale = lax.rsqrt(squares / (len(means) * features) + epsilon)

    def work(span):
        moved, biases = 0.0, bias[:, span]
        for value, top in zip(away, tops):
            moved = moved + value * top[0:1, span]
            biases = biases + top[1:2, span]
        preact = (sums(span) + moved) * scale + biases
        out[:, span] = jax.nn.gelu(preact, approximate=True).astype(jnp.bfloat16)

    columns(units, 512, work)


def activate(features, first, place, ours, moving, other, tops, bias):
    units = bias.shape[1]
    return pl.pallas_call(
        functools.partial(activate_kernel, features, first),
        in_specs=[scalars] + [whole] * 7,
        out_specs=whole,
        out_shape=jax.ShapeDtypeStruct((rows, units), jnp.bfloat16),
        compiler_params=params(24),
        cost_estimate=pl.CostEstimate(
            flops=60 * rows * units, bytes_accessed=12 * rows * units, transcendentals=rows * units
        ),
    )(place, ours, moving, other, *tops, bias)


def pass_kernel(value, *refs):
    out = refs[-1]
    out[...] = value[: out.shape[0]]


def passed(value, tokens, *before):
    return pl.pallas_call(
        pass_kernel,
        in_specs=[whole] + [anywhere] * len(before),
        out_specs=whole,
        out_shape=jax.ShapeDtypeStruct((tokens, value.shape[1]), value.dtype),
        compiler_params=params(16),
    )(value, *before)


def product_kernel(*refs):
    tiles, weight, out = refs[:-2], refs[-2], refs[-1]
    left = jnp.concatenate([tile[...] for tile in tiles])
    total = jnp.dot(left, weight[...], preferred_element_type=jnp.float32)
    out[...] = total.astype(jnp.bfloat16)


def merge_kernel(slots, earlier, place, *refs):
    done, weight, out, left = refs[0], refs[earlier], refs[-2], refs[-1]
    first = 0
    for tile in refs[earlier + 1 : -2]:
        left[first : first + tile.shape[0]] = tile[...]
        first += tile.shape[0]
    places = [(early, 8 * part + 4 * which, number) for early, (number, part, which) in slots(place[1])]

    def work(span):
        total = jnp.dot(left[...], weight[:, span], preferred_element_type=jnp.float32)
        old = new = 0
        for early, base, number in places:
            for i in range(4):
                if early:
                    first = old * rows + i * group
                    out[base + i, number, :, span] = done[first : first + group, span]
                else:
                    first = new * rows + i * group
                    out[base + i, number, :, span] = total[first : first + group].astype(jnp.bfloat16)
            old, new = old + early, new + 1 - early

    columns(weight.shape[1], 256, work)


def near_slots(core):
    out = []
    for part in range(parts):
        out += [(0, (0, part, core)), (0, (0, part, 1 - core))]
        for steps in (1, 2):
            number = 2 * steps - 1 + core
            out += [(0, (number, part, core)), (0, (number, part, 1 - core))]
        for steps in (1, 2):
            number = 2 * steps - core
            out += [(0, (number, part, 1 - core)), (0, (number, part, core))]
    return out


def far_slots(core):
    out = []
    for part in range(parts):
        out += [(1, (core, part, core)), (1, (core, part, 1 - core))]
        out += [(1, (1 - core, part, 1 - core)), (1, (1 - core, part, core))]
    for part in range(parts):
        out += [(0, (2, part, core)), (0, (2, part, 1 - core))]
    return out


def second_cost(tokens, weight):
    units, features = weight.shape
    return pl.CostEstimate(
        flops=2 * tokens * features * units,
        bytes_accessed=2 * (features * units + tokens * (features + units)),
        transcendentals=0,
    )


def second_product(tiles, weight):
    tokens = sum(tile.shape[0] for tile in tiles)
    return pl.pallas_call(
        product_kernel,
        in_specs=[whole] * (len(tiles) + 1),
        out_specs=whole,
        out_shape=jax.ShapeDtypeStruct((tokens, weight.shape[1]), jnp.bfloat16),
        compiler_params=params(24),
        cost_estimate=second_cost(tokens, weight),
    )(*tiles, weight)


def merged_product(slots, groups, place, done, tiles, weight, *before):
    tokens = sum(tile.shape[0] for tile in tiles)

    def kernel(*refs):
        skipped = len(refs) - 2 - len(before)
        merge_kernel(slots, len(done), *refs[:skipped], *refs[-2:])

    return pl.pallas_call(
        kernel,
        in_specs=[scalars] + [whole] * (len(done) + 1 + len(tiles)) + [anywhere] * len(before),
        out_specs=whole,
        out_shape=jax.ShapeDtypeStruct((16, groups, group, weight.shape[1]), jnp.bfloat16),
        scratch_shapes=[pltpu.VMEM((tokens, weight.shape[0]), jnp.bfloat16)],
        compiler_params=params(24),
        cost_estimate=second_cost(tokens, weight),
    )(place, *done, weight, *tiles, *before)


def base_kernel(tokens, bias, out):
    for i in range(tokens.shape[0]):
        out[i] = tokens[i].astype(jnp.float32) + bias[...]


def base_sum(tokens, bias):
    return pl.pallas_call(
        base_kernel,
        in_specs=[whole] * 2,
        out_specs=whole,
        out_shape=jax.ShapeDtypeStruct(tokens.shape, jnp.float32),
        compiler_params=params(16),
    )(tokens, bias)


def last_kernel(place, near, far, base, out):
    offsets = (0, -1, 1, -2, 2, -3, 3, 4)
    for slot, steps in enumerate(offsets):
        where = around(place[0], steps)
        shares, number = (near, slot) if slot < 5 else (far, slot - 5)

        def more(i, total):
            return total + shares[i, number].astype(jnp.float32)

        total = lax.fori_loop(0, shares.shape[0], more, base[where])
        out[where] = total.astype(jnp.bfloat16)


def last_sum(place, near, far, base):
    return pl.pallas_call(
        last_kernel,
        in_specs=[scalars] + [whole] * 3,
        out_specs=whole,
        out_shape=jax.ShapeDtypeStruct(base.shape, jnp.bfloat16),
        compiler_params=params(24),
    )(place, near, far, base)


def body(tokens, norm_gain, norm_bias, weight_in, bias_in, weight_out, bias_out):
    core, z = lax.axis_index("core"), lax.axis_index("z")
    place = jnp.stack([z, core]).astype(jnp.int32)
    features = tokens.shape[1]
    norm_gain, norm_bias = norm_gain.reshape(1, -1), norm_bias.reshape(1, -1)
    bias_in, bias_out = bias_in.reshape(1, -1), bias_out.reshape(1, -1)
    grouped = tokens.reshape(planes, group, features)

    def exchange(value):
        return lax.all_to_all(value, plane, 0, 0, tiled=True)

    ready = copies((4, 3, -3, 2, -2, 1, -1, 0), place, grouped)
    gathered = exchange(ready)
    mine = tops_product(norm_gain, norm_bias, weight_in, ready)
    pair = jnp.stack([mine, swap(mine)])
    near = [onward(pair, distance) for distance in (1, 2, 3)] + [onward(mine, 4)[None]]
    near = jnp.concatenate(near)
    far = swap(near)
    tops = pair, near, far

    theirs, ours = first_product(early_blocks, place, gathered, norm_gain, weight_in, far)
    theirs_later, ours_later = first_product(
        later_blocks, place, gathered, norm_gain, weight_in, theirs
    )
    theirs = swap(theirs)
    sent = [ring_sum(0, 3 * part, 3 * part, ours, theirs, theirs) for part in range(parts)]
    moving = [onward(value) for value in sent]
    for part in range(parts):
        first = 3 * part + 1
        moving[part] = onward(ring_sum(1, first, first, ours, theirs, moving[part]))
    theirs, ours = swap(theirs_later), ours_later
    hidden = []
    for part in range(parts):
        first, second = 6 * part, 4 * part
        step = moving[part]
        step = onward(ring_sum(2, first, second, ours, theirs, step))
        step = onward(ring_sum(3, first + 2, second + 2, ours, theirs, step))
        other = swap(ring_sum(4, first + 5, 0, ours, theirs, step))
        hidden.append(activate(features, first + 4, place, ours, step, other, tops, bias_in))

    base = base_sum(grouped, bias_out)
    tiles, steps = [], []
    for part in range(parts):
        step = jnp.concatenate([hidden[part], swap(hidden[part])])
        own = [step]
        for _ in range(2):
            step = onward(step)
            own.append(step)
        tiles += own + [swap(value) for value in own[1:]]
        steps.append(onward(step))
    near = merged_product(near_slots, 5, place, [], tiles, weight_out, base)
    four = [onward(passed(value, rows, near)) for value in steps]
    near = exchange(near)
    done = second_product([value for step in steps for value in (step, swap(step))], weight_out)
    four = [passed(value, rows, done) for value in four]
    far = [value for step in four for value in (step, swap(step))]
    far = merged_product(far_slots, 3, place, [done], far, weight_out)
    far = exchange(far)
    out = last_sum(place, near, far, base)
    return out.reshape(tokens.shape)


def solution(mesh):
    fine = Mesh(mesh.devices.reshape(8, 2, 4, 4), ("z", "core", "y", "x"))
    row, col = ("z", "core"), ("y", "x")
    placed = (P(col, row), P(row), P(row), P(row, col), P(col), P(col, row), P(row))
    return jax.shard_map(
        body, mesh=fine, in_specs=placed, out_specs=P(col, row), check_vma=False
    )
```

```python
import functools

import jax
import jax.numpy as jnp
from jax import lax
from jax.experimental import pallas as pl
from jax.experimental.pallas import tpu as pltpu
from jax.sharding import Mesh
from jax.sharding import PartitionSpec as P

epsilon = 1e-05
planes = 8
parts = 2
group = 8
rows = 32
plane = ("y", "x")
megabyte = 2**20
whole = pl.BlockSpec(memory_space=pltpu.VMEM)
scalars = pl.BlockSpec(memory_space=pltpu.SMEM)
anywhere = pl.BlockSpec(memory_space=pl.ANY)


def swap(value):
    return lax.ppermute(value, "core", [(0, 1), (1, 0)])


def onward(value, distance=1):
    pairs = []
    for z in range(planes):
        pairs.append((2 * z, 2 * ((z + distance) % planes)))
        pairs.append((2 * z + 1, 2 * ((z - distance) % planes) + 1))
    return lax.ppermute(value, ("z", "core"), pairs)


def around(z, steps):
    return lax.rem(z + steps + planes, planes)


def near_and_far(z, core):
    way = 1 - 2 * core
    out = [(0, core), (0, 1 - core)]
    for steps in (1, 2, 3):
        out += [(-way * steps, core), (-way * steps, 1 - core)]
    out.append((4, core))
    for steps in (1, 2, 3):
        out += [(way * steps, 1 - core), (way * steps, core)]
    out.append((4, 1 - core))
    return [2 * around(z, steps) + which for steps, which in out]


def params(size):
    return pltpu.CompilerParams(vmem_limit_bytes=size * megabyte)


def tops_kernel(gain, bias, weight, *refs):
    out = refs[-1]
    left = []
    for value in (gain[...], bias[...]):
        for _ in range(3):
            piece = value.astype(jnp.bfloat16).astype(jnp.float32)
            left.append(piece)
            value = value - piece
    left += [jnp.zeros_like(left[0])] * 10
    left = jnp.concatenate(left).astype(jnp.bfloat16)
    value = jnp.dot(left, weight[...], preferred_element_type=jnp.float32)
    out[0:1] = value[0:1] + value[1:2] + value[2:3]
    out[1:2] = value[3:4] + value[4:5] + value[5:6]


def tops_product(gain, bias, weight, *before):
    features, units = weight.shape
    step = 1536
    return pl.pallas_call(
        tops_kernel,
        grid=(units // step,),
        in_specs=[pl.BlockSpec((1, features), lambda i: (0, 0))] * 2
        + [pl.BlockSpec((features, step), lambda i: (0, i))]
        + [anywhere] * len(before),
        out_specs=pl.BlockSpec((2, step), lambda i: (0, i)),
        out_shape=jax.ShapeDtypeStruct((2, units), jnp.float32),
        compiler_params=params(24),
        cost_estimate=pl.CostEstimate(
            flops=32 * features * units, bytes_accessed=2 * features * units, transcendentals=0
        ),
    )(gain, bias, weight, *before)


def early_blocks(core):
    way = 1 - 2 * core
    theirs, ours = [], []
    for part in range(parts):
        theirs += [(4, part, 1 - core), (-3 * way, part, 1 - core), (-3 * way, part, core)]
        ours += [(4, part, core), (3 * way, part, core), (3 * way, part, 1 - core)]
    return theirs, ours


def later_blocks(core):
    way = 1 - 2 * core
    theirs, ours = [], []
    for part in range(parts):
        for steps in (2, 1):
            theirs += [(-steps * way, part, 1 - core), (-steps * way, part, core)]
            ours += [(steps * way, part, core), (steps * way, part, 1 - core)]
        ours += [(0, part, core), (0, part, 1 - core)]
    return theirs, ours


def first_kernel(choose, place, gathered, gain, weight, *refs):
    theirs, ours, left, notes = refs[-4:]
    z, core = place[0], place[1]
    features = gathered.shape[-1]
    split = theirs.shape[0]

    lane = lax.broadcasted_iota(jnp.int32, (rows, 128), 1)
    kind = lax.div(lane, 16)
    here = lane - 16 * kind == 2 * z + core
    for slot, (steps, part, which) in enumerate(sum(choose(core), [])):
        span = slice(slot * rows, (slot + 1) * rows)
        base = 8 * part + 4 * which
        block = jnp.concatenate(
            [gathered[base + i, around(z, steps)].astype(jnp.float32) for i in range(4)]
        )
        mean = jnp.sum(block, axis=1, keepdims=True) / features
        differ = block - mean
        left[span] = (differ * gain[...]).astype(jnp.bfloat16)
        note = jnp.zeros((rows, 128), jnp.float32)
        squares = jnp.sum(differ * differ, axis=1, keepdims=True)
        for first, value in ((0, mean), (3, squares)):
            rest = jnp.broadcast_to(value, (rows, 128))
            for piece in range(3):
                near = rest.astype(jnp.bfloat16).astype(jnp.float32)
                note = jnp.where(kind == first + piece, near, note)
                rest = rest - near
        notes[span] = jnp.where(here, note, 0.0).astype(jnp.bfloat16)
    theirs[:, -128:] = notes[:split]
    ours[:, -128:] = notes[split:]

    step = 768
    for first in range(0, weight.shape[1], step):
        span = slice(first, first + step)
        value = jnp.dot(left[...], weight[:, span], preferred_element_type=jnp.float32)
        theirs[:, span] = value[:split].astype(jnp.bfloat16)
        ours[:, span] = value[split:].astype(jnp.bfloat16)


def first_product(choose, place, gathered, gain, weight, *before):
    features, units = weight.shape
    split, rest = (rows * len(blocks) for blocks in choose(0))
    tokens = split + rest
    return pl.pallas_call(
        functools.partial(first_kernel, choose),
        in_specs=[scalars] + [whole] * 3 + [anywhere] * len(before),
        out_specs=[whole, whole],
        out_shape=[
            jax.ShapeDtypeStruct((split, units + 128), jnp.bfloat16),
            jax.ShapeDtypeStruct((rest, units + 128), jnp.bfloat16),
        ],
        scratch_shapes=[
            pltpu.VMEM((tokens, features), jnp.bfloat16),
            pltpu.VMEM((tokens, 128), jnp.bfloat16),
        ],
        compiler_params=params(24),
        cost_estimate=pl.CostEstimate(
            flops=2 * tokens * features * units,
            bytes_accessed=2 * (features * units + tokens * (features + units)),
            transcendentals=0,
        ),
    )(place, gathered, gain, weight, *before)


def columns(wide, step, work):
    def chunk(number, carry):
        work(pl.ds(pl.multiple_of(number * step, step), step))
        return carry

    lax.fori_loop(0, wide // step, chunk, 0)


def sum_kernel(number, first, second, ours, theirs, moving, *refs):
    out = refs[-1]
    size = out.shape[0]

    def work(span):
        total = ours[first * rows : first * rows + size, span].astype(jnp.float32)
        if number == 4:
            total = total + moving[rows:, span].astype(jnp.float32)
        else:
            share = theirs[second * rows : second * rows + size, span]
            total = total + share.astype(jnp.float32)
        if number in (2, 3):
            total = total + moving[:, span].astype(jnp.float32)
        if number == 1:
            near = total[:rows] + moving[:, span].astype(jnp.float32)
            out[:rows, span] = near.astype(jnp.bfloat16)
            out[rows:, span] = total[rows:].astype(jnp.bfloat16)
        else:
            out[:, span] = total.astype(jnp.bfloat16)

    columns(out.shape[1], 640, work)


def ring_sum(number, first, second, ours, theirs, moving, *before):
    shape = (rows if number in (0, 4) else 2 * rows, ours.shape[1])
    return pl.pallas_call(
        functools.partial(sum_kernel, number, first, second),
        in_specs=[whole] * 3 + [anywhere] * len(before),
        out_specs=whole,
        out_shape=jax.ShapeDtypeStruct(shape, jnp.bfloat16),
        compiler_params=params(16),
        cost_estimate=pl.CostEstimate(
            flops=3 * shape[0] * shape[1], bytes_accessed=8 * shape[0] * shape[1], transcendentals=0
        ),
    )(ours, theirs, moving, *before)


def activate_kernel(features, first, place, ours, moving, other, *refs):
    tops, bias, out = refs[:-2], refs[-2], refs[-1]
    units = out.shape[1]

    def sums(span):
        total = ours[first * rows : (first + 1) * rows, span].astype(jnp.float32)
        total = total + moving[:rows, span].astype(jnp.float32)
        return total + other[:, span].astype(jnp.float32)

    notes = sums(pl.ds(units, 128))
    lane = lax.broadcasted_iota(jnp.int32, (rows, 128), 1)
    kind = lax.div(lane, 16)
    lane = lane - 16 * kind
    tops = [top.at[i] for top in tops for i in range(top.shape[0])]
    means, squares = [], 0.0
    for number in near_and_far(place[0], place[1]):
        mine = jnp.where(lane == number, notes, 0.0)
        means.append(jnp.sum(jnp.where(kind < 3, mine, 0.0), axis=1, keepdims=True))
        squares = squares + jnp.sum(jnp.where(kind >= 3, mine, 0.0), axis=1, keepdims=True)
    center = sum(means) / len(means)
    away = [mean - center for mean in means]
    for value in away:
        squares = squares + features * value * value
    scale = lax.rsqrt(squares / (len(means) * features) + epsilon)

    def work(span):
        moved, biases = 0.0, bias[:, span]
        for value, top in zip(away, tops):
            moved = moved + value * top[0:1, span]
            biases = biases + top[1:2, span]
        preact = (sums(span) + moved) * scale + biases
        out[:, span] = jax.nn.gelu(preact, approximate=True).astype(jnp.bfloat16)

    columns(units, 512, work)


def activate(features, first, place, ours, moving, other, tops, bias):
    units = bias.shape[1]
    return pl.pallas_call(
        functools.partial(activate_kernel, features, first),
        in_specs=[scalars] + [whole] * 7,
        out_specs=whole,
        out_shape=jax.ShapeDtypeStruct((rows, units), jnp.bfloat16),
        compiler_params=params(24),
        cost_estimate=pl.CostEstimate(
            flops=60 * rows * units, bytes_accessed=12 * rows * units, transcendentals=rows * units
        ),
    )(place, ours, moving, other, *tops, bias)


def pass_kernel(value, *refs):
    out = refs[-1]
    out[...] = value[: out.shape[0]]


def passed(value, tokens, *before):
    return pl.pallas_call(
        pass_kernel,
        in_specs=[whole] + [anywhere] * len(before),
        out_specs=whole,
        out_shape=jax.ShapeDtypeStruct((tokens, value.shape[1]), value.dtype),
        compiler_params=params(16),
    )(value, *before)


def product_kernel(*refs):
    tiles, weight, out, held = refs[:-3], refs[-3], refs[-2], refs[-1]
    left = jnp.concatenate([tile[...] for tile in tiles])
    total = jnp.dot(left, weight[...], preferred_element_type=jnp.float32)
    out[...] = total.astype(jnp.bfloat16)
    held[...] = weight[...]


def merge_kernel(slots, earlier, place, *refs):
    done, weight, out, left = refs[0], refs[earlier], refs[-2], refs[-1]
    first = 0
    for tile in refs[earlier + 1 : -2]:
        left[first : first + tile.shape[0]] = tile[...]
        first += tile.shape[0]
    places = [(early, 8 * part + 4 * which, number) for early, (number, part, which) in slots(place[1])]

    def work(span):
        total = jnp.dot(left[...], weight[:, span], preferred_element_type=jnp.float32)
        old = new = 0
        for early, base, number in places:
            for i in range(4):
                if early:
                    first = old * rows + i * group
                    out[base + i, number, :, span] = done[first : first + group, span]
                else:
                    first = new * rows + i * group
                    out[base + i, number, :, span] = total[first : first + group].astype(jnp.bfloat16)
            old, new = old + early, new + 1 - early

    columns(weight.shape[1], 256, work)


def near_slots(core):
    out = []
    for part in range(parts):
        out += [(0, (0, part, core)), (0, (0, part, 1 - core))]
        for steps in (1, 2):
            number = 2 * steps - 1 + core
            out += [(0, (number, part, core)), (0, (number, part, 1 - core))]
        for steps in (1, 2):
            number = 2 * steps - core
            out += [(0, (number, part, 1 - core)), (0, (number, part, core))]
    return out


def far_slots(core):
    out = []
    for part in range(parts):
        out += [(1, (core, part, core)), (1, (core, part, 1 - core))]
        out += [(1, (1 - core, part, 1 - core)), (1, (1 - core, part, core))]
    for part in range(parts):
        out += [(0, (2, part, core)), (0, (2, part, 1 - core))]
    return out


def second_cost(tokens, weight):
    units, features = weight.shape
    return pl.CostEstimate(
        flops=2 * tokens * features * units,
        bytes_accessed=2 * (features * units + tokens * (features + units)),
        transcendentals=0,
    )


def second_product(tiles, weight):
    tokens = sum(tile.shape[0] for tile in tiles)
    return pl.pallas_call(
        product_kernel,
        in_specs=[whole] * (len(tiles) + 1),
        out_specs=[whole, whole],
        out_shape=[
            jax.ShapeDtypeStruct((tokens, weight.shape[1]), jnp.bfloat16),
            jax.ShapeDtypeStruct(weight.shape, weight.dtype),
        ],
        compiler_params=params(24),
        cost_estimate=second_cost(tokens, weight),
    )(*tiles, weight)


def merged_product(slots, groups, place, done, tiles, weight, *before):
    tokens = sum(tile.shape[0] for tile in tiles)

    def kernel(*refs):
        skipped = len(refs) - 2 - len(before)
        merge_kernel(slots, len(done), *refs[:skipped], *refs[-2:])

    return pl.pallas_call(
        kernel,
        in_specs=[scalars] + [whole] * (len(done) + 1 + len(tiles)) + [anywhere] * len(before),
        out_specs=whole,
        out_shape=jax.ShapeDtypeStruct((16, groups, group, weight.shape[1]), jnp.bfloat16),
        scratch_shapes=[pltpu.VMEM((tokens, weight.shape[0]), jnp.bfloat16)],
        compiler_params=params(24),
        cost_estimate=second_cost(tokens, weight),
    )(place, *done, weight, *tiles, *before)


def base_kernel(tokens, bias, out):
    for i in range(tokens.shape[0]):
        out[i] = tokens[i].astype(jnp.float32) + bias[...]


def base_sum(tokens, bias):
    return pl.pallas_call(
        base_kernel,
        in_specs=[whole] * 2,
        out_specs=whole,
        out_shape=jax.ShapeDtypeStruct(tokens.shape, jnp.float32),
        compiler_params=params(16),
    )(tokens, bias)


def last_kernel(place, near, far, base, out):
    offsets = (0, -1, 1, -2, 2, -3, 3, 4)
    for slot, steps in enumerate(offsets):
        where = around(place[0], steps)
        shares, number = (near, slot) if slot < 5 else (far, slot - 5)

        def more(i, total):
            return total + shares[i, number].astype(jnp.float32)

        total = lax.fori_loop(0, shares.shape[0], more, base[where])
        out[where] = total.astype(jnp.bfloat16)


def last_sum(place, near, far, base):
    return pl.pallas_call(
        last_kernel,
        in_specs=[scalars] + [whole] * 3,
        out_specs=whole,
        out_shape=jax.ShapeDtypeStruct(base.shape, jnp.bfloat16),
        compiler_params=params(24),
    )(place, near, far, base)


def body(tokens, norm_gain, norm_bias, weight_in, bias_in, weight_out, bias_out):
    core, z = lax.axis_index("core"), lax.axis_index("z")
    place = jnp.stack([z, core]).astype(jnp.int32)
    features = tokens.shape[1]
    norm_gain, norm_bias = norm_gain.reshape(1, -1), norm_bias.reshape(1, -1)
    bias_in, bias_out = bias_in.reshape(1, -1), bias_out.reshape(1, -1)
    grouped = tokens.reshape(planes, group, features)

    def exchange(value):
        return lax.all_to_all(value, plane, 0, 0, tiled=True)

    ready = jnp.broadcast_to(grouped[None], (16,) + grouped.shape)
    gathered = exchange(ready)
    mine = tops_product(norm_gain, norm_bias, weight_in, ready)
    pair = jnp.stack([mine, swap(mine)])
    near = [onward(pair, distance) for distance in (1, 2, 3)] + [onward(mine, 4)[None]]
    near = jnp.concatenate(near)
    far = swap(near)
    tops = pair, near, far

    theirs, ours = first_product(early_blocks, place, gathered, norm_gain, weight_in, far)
    theirs_later, ours_later = first_product(
        later_blocks, place, gathered, norm_gain, weight_in, theirs
    )
    theirs = swap(theirs)
    sent = [ring_sum(0, 3 * part, 3 * part, ours, theirs, theirs) for part in range(parts)]
    moving = [onward(value) for value in sent]
    for part in range(parts):
        first = 3 * part + 1
        moving[part] = onward(ring_sum(1, first, first, ours, theirs, moving[part]))
    theirs, ours = swap(theirs_later), ours_later
    hidden = []
    for part in range(parts):
        first, second = 6 * part, 4 * part
        step = moving[part]
        step = onward(ring_sum(2, first, second, ours, theirs, step))
        step = onward(ring_sum(3, first + 2, second + 2, ours, theirs, step))
        other = swap(ring_sum(4, first + 5, 0, ours, theirs, step))
        value = activate(features, first + 4, place, ours, step, other, tops, bias_in)
        hidden.append(jnp.concatenate([value, swap(value)]))

    base = base_sum(grouped, bias_out)
    tiles, steps = [], []
    for part in range(parts):
        step = hidden[part]
        own = [step]
        for _ in range(2):
            step = onward(step)
            own.append(step)
        tiles += own + [swap(value) for value in own[1:]]
        steps.append(onward(step))
    near = merged_product(near_slots, 5, place, [], tiles, weight_out, base)
    four = [onward(passed(value, rows, near)) for value in steps]
    near = exchange(near)
    done, held = second_product(
        [value for step in steps for value in (step, swap(step))], weight_out
    )
    four = [passed(value, rows, done) for value in four]
    far = [value for step in four for value in (step, swap(step))]
    far = merged_product(far_slots, 3, place, [done], far, held)
    far = exchange(far)
    out = last_sum(place, near, far, base)
    return out.reshape(tokens.shape)


def solution(mesh):
    fine = Mesh(mesh.devices.reshape(8, 2, 4, 4), ("z", "core", "y", "x"))
    row, col = ("z", "core"), ("y", "x")
    placed = (P(col, row), P(row), P(row), P(row, col), P(col), P(col, row), P(row))
    return jax.shard_map(
        body, mesh=fine, in_specs=placed, out_specs=P(col, row), check_vma=False
    )
```

```python
import functools

import jax
import jax.numpy as jnp
from jax import lax
from jax.experimental import pallas as pl
from jax.experimental.pallas import tpu as pltpu
from jax.sharding import Mesh
from jax.sharding import PartitionSpec as P

epsilon = 1e-05
planes = 8
parts = 2
group = 8
rows = 32
plane = ("y", "x")
megabyte = 2**20
whole = pl.BlockSpec(memory_space=pltpu.VMEM)
scalars = pl.BlockSpec(memory_space=pltpu.SMEM)
anywhere = pl.BlockSpec(memory_space=pl.ANY)


def swap(value):
    return lax.ppermute(value, "core", [(0, 1), (1, 0)])


def onward(value, distance=1):
    pairs = []
    for z in range(planes):
        pairs.append((2 * z, 2 * ((z + distance) % planes)))
        pairs.append((2 * z + 1, 2 * ((z - distance) % planes) + 1))
    return lax.ppermute(value, ("z", "core"), pairs)


def around(z, steps):
    return lax.rem(z + steps + planes, planes)


def near_and_far(z, core):
    way = 1 - 2 * core
    out = [(0, core), (0, 1 - core)]
    for steps in (1, 2, 3):
        out += [(-way * steps, core), (-way * steps, 1 - core)]
    out.append((4, core))
    for steps in (1, 2, 3):
        out += [(way * steps, 1 - core), (way * steps, core)]
    out.append((4, 1 - core))
    return [2 * around(z, steps) + which for steps, which in out]


def params(size):
    return pltpu.CompilerParams(vmem_limit_bytes=size * megabyte)


def tops_kernel(gain, bias, weight, *refs):
    out = refs[-1]
    left = []
    for value in (gain[...], bias[...]):
        for _ in range(3):
            piece = value.astype(jnp.bfloat16).astype(jnp.float32)
            left.append(piece)
            value = value - piece
    left += [jnp.zeros_like(left[0])] * 10
    left = jnp.concatenate(left).astype(jnp.bfloat16)
    value = jnp.dot(left, weight[...], preferred_element_type=jnp.float32)
    out[0:1] = value[0:1] + value[1:2] + value[2:3]
    out[1:2] = value[3:4] + value[4:5] + value[5:6]


def tops_product(gain, bias, weight, *before):
    features, units = weight.shape
    step = 1536
    return pl.pallas_call(
        tops_kernel,
        grid=(units // step,),
        in_specs=[pl.BlockSpec((1, features), lambda i: (0, 0))] * 2
        + [pl.BlockSpec((features, step), lambda i: (0, i))]
        + [anywhere] * len(before),
        out_specs=pl.BlockSpec((2, step), lambda i: (0, i)),
        out_shape=jax.ShapeDtypeStruct((2, units), jnp.float32),
        compiler_params=params(24),
        cost_estimate=pl.CostEstimate(
            flops=32 * features * units, bytes_accessed=2 * features * units, transcendentals=0
        ),
    )(gain, bias, weight, *before)


def early_blocks(core):
    way = 1 - 2 * core
    theirs, ours = [], []
    for part in range(parts):
        theirs += [(4, part, 1 - core), (-3 * way, part, 1 - core), (-3 * way, part, core)]
        ours += [(4, part, core), (3 * way, part, core), (3 * way, part, 1 - core)]
    return theirs, ours


def later_blocks(core):
    way = 1 - 2 * core
    theirs, ours = [], []
    for part in range(parts):
        for steps in (2, 1):
            theirs += [(-steps * way, part, 1 - core), (-steps * way, part, core)]
            ours += [(steps * way, part, core), (steps * way, part, 1 - core)]
        ours += [(0, part, core), (0, part, 1 - core)]
    return theirs, ours


def first_kernel(choose, place, gathered, gain, weight, *refs):
    theirs, ours, left, notes = refs[-4:]
    z, core = place[0], place[1]
    features = gathered.shape[-1]
    split = theirs.shape[0]

    lane = lax.broadcasted_iota(jnp.int32, (rows, 128), 1)
    kind = lax.div(lane, 16)
    here = lane - 16 * kind == 2 * z + core
    for slot, (steps, part, which) in enumerate(sum(choose(core), [])):
        span = slice(slot * rows, (slot + 1) * rows)
        base = 8 * part + 4 * which
        block = jnp.concatenate(
            [gathered[base + i, around(z, steps)].astype(jnp.float32) for i in range(4)]
        )
        mean = jnp.sum(block, axis=1, keepdims=True) / features
        differ = block - mean
        left[span] = (differ * gain[...]).astype(jnp.bfloat16)
        note = jnp.zeros((rows, 128), jnp.float32)
        squares = jnp.sum(differ * differ, axis=1, keepdims=True)
        for first, value in ((0, mean), (3, squares)):
            rest = jnp.broadcast_to(value, (rows, 128))
            for piece in range(3):
                near = rest.astype(jnp.bfloat16).astype(jnp.float32)
                note = jnp.where(kind == first + piece, near, note)
                rest = rest - near
        notes[span] = jnp.where(here, note, 0.0).astype(jnp.bfloat16)
    theirs[:, -128:] = notes[:split]
    ours[:, -128:] = notes[split:]

    step = 768
    for first in range(0, weight.shape[1], step):
        span = slice(first, first + step)
        value = jnp.dot(left[...], weight[:, span], preferred_element_type=jnp.float32)
        theirs[:, span] = value[:split].astype(jnp.bfloat16)
        ours[:, span] = value[split:].astype(jnp.bfloat16)


def first_product(choose, place, gathered, gain, weight, *before):
    features, units = weight.shape
    split, rest = (rows * len(blocks) for blocks in choose(0))
    tokens = split + rest
    return pl.pallas_call(
        functools.partial(first_kernel, choose),
        in_specs=[scalars] + [whole] * 3 + [anywhere] * len(before),
        out_specs=[whole, whole],
        out_shape=[
            jax.ShapeDtypeStruct((split, units + 128), jnp.bfloat16),
            jax.ShapeDtypeStruct((rest, units + 128), jnp.bfloat16),
        ],
        scratch_shapes=[
            pltpu.VMEM((tokens, features), jnp.bfloat16),
            pltpu.VMEM((tokens, 128), jnp.bfloat16),
        ],
        compiler_params=params(24),
        cost_estimate=pl.CostEstimate(
            flops=2 * tokens * features * units,
            bytes_accessed=2 * (features * units + tokens * (features + units)),
            transcendentals=0,
        ),
    )(place, gathered, gain, weight, *before)


def columns(wide, step, work):
    def chunk(number, carry):
        work(pl.ds(pl.multiple_of(number * step, step), step))
        return carry

    lax.fori_loop(0, wide // step, chunk, 0)


def sum_kernel(number, first, second, ours, theirs, moving, *refs):
    out = refs[-1]
    size = out.shape[0]

    def work(span):
        total = ours[first * rows : first * rows + size, span].astype(jnp.float32)
        if number == 4:
            total = total + moving[rows:, span].astype(jnp.float32)
        else:
            share = theirs[second * rows : second * rows + size, span]
            total = total + share.astype(jnp.float32)
        if number in (2, 3):
            total = total + moving[:, span].astype(jnp.float32)
        if number == 1:
            near = total[:rows] + moving[:, span].astype(jnp.float32)
            out[:rows, span] = near.astype(jnp.bfloat16)
            out[rows:, span] = total[rows:].astype(jnp.bfloat16)
        else:
            out[:, span] = total.astype(jnp.bfloat16)

    columns(out.shape[1], 640, work)


def ring_sum(number, first, second, ours, theirs, moving, *before):
    shape = (rows if number in (0, 4) else 2 * rows, ours.shape[1])
    return pl.pallas_call(
        functools.partial(sum_kernel, number, first, second),
        in_specs=[whole] * 3 + [anywhere] * len(before),
        out_specs=whole,
        out_shape=jax.ShapeDtypeStruct(shape, jnp.bfloat16),
        compiler_params=params(16),
        cost_estimate=pl.CostEstimate(
            flops=3 * shape[0] * shape[1], bytes_accessed=8 * shape[0] * shape[1], transcendentals=0
        ),
    )(ours, theirs, moving, *before)


def activate_kernel(features, first, place, ours, moving, other, *refs):
    tops, bias, out = refs[:-2], refs[-2], refs[-1]
    units = out.shape[1]

    def sums(span):
        total = ours[first * rows : (first + 1) * rows, span].astype(jnp.float32)
        total = total + moving[:rows, span].astype(jnp.float32)
        return total + other[:, span].astype(jnp.float32)

    notes = sums(pl.ds(units, 128))
    lane = lax.broadcasted_iota(jnp.int32, (rows, 128), 1)
    kind = lax.div(lane, 16)
    lane = lane - 16 * kind
    tops = [top.at[i] for top in tops for i in range(top.shape[0])]
    means, squares = [], 0.0
    for number in near_and_far(place[0], place[1]):
        mine = jnp.where(lane == number, notes, 0.0)
        means.append(jnp.sum(jnp.where(kind < 3, mine, 0.0), axis=1, keepdims=True))
        squares = squares + jnp.sum(jnp.where(kind >= 3, mine, 0.0), axis=1, keepdims=True)
    center = sum(means) / len(means)
    away = [mean - center for mean in means]
    for value in away:
        squares = squares + features * value * value
    scale = lax.rsqrt(squares / (len(means) * features) + epsilon)

    def work(span):
        moved, biases = 0.0, bias[:, span]
        for value, top in zip(away, tops):
            moved = moved + value * top[0:1, span]
            biases = biases + top[1:2, span]
        preact = (sums(span) + moved) * scale + biases
        out[:, span] = jax.nn.gelu(preact, approximate=True).astype(jnp.bfloat16)

    columns(units, 512, work)


def activate(features, first, place, ours, moving, other, tops, bias):
    units = bias.shape[1]
    return pl.pallas_call(
        functools.partial(activate_kernel, features, first),
        in_specs=[scalars] + [whole] * 7,
        out_specs=whole,
        out_shape=jax.ShapeDtypeStruct((rows, units), jnp.bfloat16),
        compiler_params=params(24),
        cost_estimate=pl.CostEstimate(
            flops=60 * rows * units, bytes_accessed=12 * rows * units, transcendentals=rows * units
        ),
    )(place, ours, moving, other, *tops, bias)


def pass_kernel(value, *refs):
    out = refs[-1]
    out[...] = value[: out.shape[0]]


def passed(value, tokens, *before):
    return pl.pallas_call(
        pass_kernel,
        in_specs=[whole] + [anywhere] * len(before),
        out_specs=whole,
        out_shape=jax.ShapeDtypeStruct((tokens, value.shape[1]), value.dtype),
        compiler_params=params(16),
    )(value, *before)


def product_kernel(*refs):
    tiles, weight, out, held = refs[:-3], refs[-3], refs[-2], refs[-1]
    left = jnp.concatenate([tile[...] for tile in tiles])

    def work(span):
        total = jnp.dot(left, weight[:, span], preferred_element_type=jnp.float32)
        out[:, span] = total.astype(jnp.bfloat16)
        held[:, span] = weight[:, span]

    columns(weight.shape[1], 256, work)


def merge_kernel(slots, earlier, place, *refs):
    done, weight, out, left = refs[0], refs[earlier], refs[-2], refs[-1]
    first = 0
    for tile in refs[earlier + 1 : -2]:
        left[first : first + tile.shape[0]] = tile[...]
        first += tile.shape[0]
    places = [(early, 8 * part + 4 * which, number) for early, (number, part, which) in slots(place[1])]

    def work(span):
        total = jnp.dot(left[...], weight[:, span], preferred_element_type=jnp.float32)
        old = new = 0
        for early, base, number in places:
            for i in range(4):
                if early:
                    first = old * rows + i * group
                    out[base + i, number, :, span] = done[first : first + group, span]
                else:
                    first = new * rows + i * group
                    out[base + i, number, :, span] = total[first : first + group].astype(jnp.bfloat16)
            old, new = old + early, new + 1 - early

    columns(weight.shape[1], 256 if earlier else weight.shape[1], work)


def near_slots(core):
    out = []
    for part in range(parts):
        out += [(0, (0, part, core)), (0, (0, part, 1 - core))]
        for steps in (1, 2):
            number = 2 * steps - 1 + core
            out += [(0, (number, part, core)), (0, (number, part, 1 - core))]
        for steps in (1, 2):
            number = 2 * steps - core
            out += [(0, (number, part, 1 - core)), (0, (number, part, core))]
    return out


def far_slots(core):
    out = []
    for part in range(parts):
        out += [(1, (core, part, core)), (1, (core, part, 1 - core))]
        out += [(1, (1 - core, part, 1 - core)), (1, (1 - core, part, core))]
    for part in range(parts):
        out += [(0, (2, part, core)), (0, (2, part, 1 - core))]
    return out


def second_cost(tokens, weight):
    units, features = weight.shape
    return pl.CostEstimate(
        flops=2 * tokens * features * units,
        bytes_accessed=2 * (features * units + tokens * (features + units)),
        transcendentals=0,
    )


def second_product(tiles, weight):
    tokens = sum(tile.shape[0] for tile in tiles)
    return pl.pallas_call(
        product_kernel,
        in_specs=[whole] * (len(tiles) + 1),
        out_specs=[whole, whole],
        out_shape=[
            jax.ShapeDtypeStruct((tokens, weight.shape[1]), jnp.bfloat16),
            jax.ShapeDtypeStruct(weight.shape, weight.dtype),
        ],
        compiler_params=params(24),
        cost_estimate=second_cost(tokens, weight),
    )(*tiles, weight)


def merged_product(slots, groups, place, done, tiles, weight, *before):
    tokens = sum(tile.shape[0] for tile in tiles)

    def kernel(*refs):
        skipped = len(refs) - 2 - len(before)
        merge_kernel(slots, len(done), *refs[:skipped], *refs[-2:])

    return pl.pallas_call(
        kernel,
        in_specs=[scalars] + [whole] * (len(done) + 1 + len(tiles)) + [anywhere] * len(before),
        out_specs=whole,
        out_shape=jax.ShapeDtypeStruct((16, groups, group, weight.shape[1]), jnp.bfloat16),
        scratch_shapes=[pltpu.VMEM((tokens, weight.shape[0]), jnp.bfloat16)],
        compiler_params=params(24),
        cost_estimate=second_cost(tokens, weight),
    )(place, *done, weight, *tiles, *before)


def base_kernel(tokens, bias, out):
    for i in range(tokens.shape[0]):
        out[i] = tokens[i].astype(jnp.float32) + bias[...]


def base_sum(tokens, bias):
    return pl.pallas_call(
        base_kernel,
        in_specs=[whole] * 2,
        out_specs=whole,
        out_shape=jax.ShapeDtypeStruct(tokens.shape, jnp.float32),
        compiler_params=params(16),
    )(tokens, bias)


def last_kernel(place, near, far, base, out):
    offsets = (0, -1, 1, -2, 2, -3, 3, 4)
    where = [around(place[0], steps) for steps in offsets]

    def more(i, totals):
        shares = [near[i, slot] for slot in range(5)] + [far[i, slot] for slot in range(3)]
        return tuple(total + share.astype(jnp.float32) for total, share in zip(totals, shares))

    totals = lax.fori_loop(0, near.shape[0], more, tuple(base[number] for number in where))
    for number, total in zip(where, totals):
        out[number] = total.astype(jnp.bfloat16)


def last_sum(place, near, far, base):
    return pl.pallas_call(
        last_kernel,
        in_specs=[scalars] + [whole] * 3,
        out_specs=whole,
        out_shape=jax.ShapeDtypeStruct(base.shape, jnp.bfloat16),
        compiler_params=params(24),
    )(place, near, far, base)


def body(tokens, norm_gain, norm_bias, weight_in, bias_in, weight_out, bias_out):
    core, z = lax.axis_index("core"), lax.axis_index("z")
    place = jnp.stack([z, core]).astype(jnp.int32)
    features = tokens.shape[1]
    norm_gain, norm_bias = norm_gain.reshape(1, -1), norm_bias.reshape(1, -1)
    bias_in, bias_out = bias_in.reshape(1, -1), bias_out.reshape(1, -1)
    grouped = tokens.reshape(planes, group, features)

    def exchange(value):
        return lax.all_to_all(value, plane, 0, 0, tiled=True)

    ready = jnp.broadcast_to(grouped[None], (16,) + grouped.shape)
    gathered = exchange(ready)
    mine = tops_product(norm_gain, norm_bias, weight_in, ready)
    pair = jnp.stack([mine, swap(mine)])
    near = [onward(pair, distance) for distance in (1, 2, 3)] + [onward(mine, 4)[None]]
    near = jnp.concatenate(near)
    far = swap(near)
    tops = pair, near, far

    theirs, ours = first_product(early_blocks, place, gathered, norm_gain, weight_in, far)
    theirs_later, ours_later = first_product(
        later_blocks, place, gathered, norm_gain, weight_in, theirs
    )
    theirs = swap(theirs)
    sent = [ring_sum(0, 3 * part, 3 * part, ours, theirs, theirs) for part in range(parts)]
    moving = [onward(value) for value in sent]
    for part in range(parts):
        first = 3 * part + 1
        moving[part] = onward(ring_sum(1, first, first, ours, theirs, moving[part]))
    theirs, ours = swap(theirs_later), ours_later
    hidden = []
    for part in range(parts):
        first, second = 6 * part, 4 * part
        step = moving[part]
        step = onward(ring_sum(2, first, second, ours, theirs, step))
        step = onward(ring_sum(3, first + 2, second + 2, ours, theirs, step))
        other = swap(ring_sum(4, first + 5, 0, ours, theirs, step))
        value = activate(features, first + 4, place, ours, step, other, tops, bias_in)
        hidden.append(jnp.concatenate([value, swap(value)]))

    base = base_sum(grouped, bias_out)
    tiles, steps = [], []
    for part in range(parts):
        step = hidden[part]
        own = [step]
        for _ in range(2):
            step = onward(step)
            own.append(step)
        tiles += own + [swap(value) for value in own[1:]]
        steps.append(onward(step))
    near = merged_product(near_slots, 5, place, [], tiles, weight_out, base)
    four = [onward(passed(value, rows, near)) for value in steps]
    near = exchange(near)
    done, held = second_product(
        [value for step in steps for value in (step, swap(step))], weight_out
    )
    four = [passed(value, rows, done) for value in four]
    far = [value for step in four for value in (step, swap(step))]
    far = merged_product(far_slots, 3, place, [done], far, held)
    far = exchange(far)
    out = last_sum(place, near, far, base)
    return out.reshape(tokens.shape)


def solution(mesh):
    fine = Mesh(mesh.devices.reshape(8, 2, 4, 4), ("z", "core", "y", "x"))
    row, col = ("z", "core"), ("y", "x")
    placed = (P(col, row), P(row), P(row), P(row, col), P(col), P(col, row), P(row))
    return jax.shard_map(
        body, mesh=fine, in_specs=placed, out_specs=P(col, row), check_vma=False
    )
```
